768 devices in a mesh: replica: 48 (over y_hi, z), node: 4 (over x), local: 4 (over y_lo, core).
Axes of the slice: x: 4, y: 8 (y_hi: 4, y_lo: 2; y = y_hi * 2 + y_lo), z: 12, core: 2. Of those that a mesh axis runs over, the one named last changes fastest.
Arguments:
- token_grads: bfloat16 [24576, 3840], P(('replica', 'local'), 'node'), may hold values from -6 to 6
- routes: int32 [24576, 2], P(('replica', 'local')), may hold values from 0 to 3, all different within a row; in each aligned block of 128 rows (0 to 127, 128 to 255, ...) at most 72 rows name the same one
- gates: bfloat16 [24576, 2], P(('replica', 'local')), may hold values from 0.19921875 to 1
- expert_inputs: bfloat16 [48, 4, 4, 72, 3840], P('replica', 'local', None, None, 'node'), may hold values from -6 to 6
- gate_pre: bfloat16 [48, 4, 4, 72, 1024], P('replica', 'local'), may hold values from -8 to 8
- up_pre: bfloat16 [48, 4, 4, 72, 1024], P('replica', 'local'), may hold values from -6 to 6
- w_gate: bfloat16 [4, 3840, 1024], P('local', 'node'), may hold values from -0.09375 to 0.09375
- w_up: bfloat16 [4, 3840, 1024], P('local', 'node'), may hold values from -0.09375 to 0.09375
- w_down: bfloat16 [4, 1024, 3840], P('local', None, 'node'), may hold values from -0.1875 to 0.1875
Outputs:
- input_grads: bfloat16 [24576, 3840], P(('replica', 'local'), 'node')
- gate_grads: bfloat16 [24576, 2], P(('replica', 'local'))
- gate_weight_grads: float32 [4, 4, 7680, 128], P('local', 'node', 'replica')
- up_weight_grads: float32 [4, 4, 7680, 128], P('local', 'node', 'replica')
The draws below stay inside these ranges and needn't reach their ends.
Inputs may be any that keep to these rules, and one draw needn't show every extreme that they name: `routes`: each token names 2 different experts. Among the tokens of one device no expert is named more than 72 times, a bound that some block reaches.
All inputs are finite; a program needn't handle non-finite values.
Results may differ from the reference program's by a relative error of at most 0.022.
Values may be sent and summed in bfloat16 or wider, within the bound.
No kernel may reach another device: no remote copies, remote signals or barrier semaphores. Data moves between devices by JAX's collectives and lax.ppermute only.
A program may use at most 64 MiB of HBM per device.

```python
import math
import jax
import jax.numpy as jnp
import numpy as np
from jax import lax

D = 3840
FF = 1024
TOP = 2
TOK_DEV = 128
EXPERTS = 4
CAP = 72
TOKENS = 24576
N_REPLICA = 48
N_NODE = 4
N_LOCAL = 4


def level_of(rng, shape, split, low, largest):
    def one(dim, blocks):
        draws = jax.random.uniform(jax.random.fold_in(jax.random.fold_in(rng, 6), dim), (blocks,), jnp.float32, low / len(split), largest / len(split))
        return jnp.repeat(jnp.exp(draws), shape[dim] // blocks).reshape((-1,) + (1,) * (len(shape) - dim - 1))

    loudness = one(*split[0])
    for cut in split[1:]:
        loudness = loudness * one(*cut)
    return loudness


def deal_out(stream_key, own, number, rows, number_of, top, reach, skew):
    order = jax.random.permutation(stream_key, number_of)
    heavy_load, ordinary = portions_of(number_of, rows * top, reach, skew, True), portions_of(number_of, rows * top, reach, skew, False)
    places = jnp.arange(number_of)

    def named(tallies, turn):
        used = int((tallies > 0).sum())
        fixed = max(1, used // 4)
        moved = fixed + (places - fixed + turn * (used - fixed)) % max(1, number_of - fixed)
        return jnp.zeros((number_of,), jnp.int32).at[order[jnp.where(places < fixed, places, moved)]].set(jnp.asarray(tallies, jnp.int32))

    tallies = jnp.where(number % 4 == 0, named(heavy_load, number // 4), named(ordinary, number - number // 4 - 1))
    mixed = jax.random.permutation(jax.random.fold_in(own, 3), number_of)
    source_of, taker = mixed[0:number_of // 2 * 2:2], mixed[1:number_of // 2 * 2:2]
    slack = jnp.minimum(tallies[source_of] - 1, reach - tallies[taker]) // 2
    slack = jnp.where((source_of == order[0]) | (taker == order[0]) | (tallies[taker] == 0), 0, jnp.maximum(slack, 0))
    moved = jax.random.randint(jax.random.fold_in(own, 4), (number_of // 2,), 0, 1 << 20) % (slack + 1)
    tallies = tallies.at[source_of].add(-moved).at[taker].add(moved)
    items = jnp.searchsorted(jnp.cumsum(tallies), jnp.arange(rows * top), side="right").astype(jnp.int32)
    table = items.reshape(top, rows).T
    table = table[jax.random.permutation(jax.random.fold_in(own, 1), rows)]
    turn = jax.random.randint(jax.random.fold_in(own, 2), (rows, 1), 0, top)
    return jnp.take_along_axis(table, (jnp.arange(top)[None, :] + turn) % top, axis=1)


def portions_of(count, total, bound, lean, full):
    loads = [(1 << 20) // math.isqrt(standing ** lean) + 1 for standing in range(1, count + 1)]
    largest = bound if full else min(bound, max(-(-total // count), total * loads[0] // sum(loads)))
    least = 1 if total - largest >= count - 1 else 0
    counts, spare = [largest] + [least] * (count - 1), total - largest - least * (count - 1)
    while spare > 0:
        free = [i for i in range(1, count) if counts[i] < largest] or [i for i in range(1, count) if counts[i] < bound]
        mass, budget = sum([loads[i] for i in free]), spare
        for i in free:
            more = min(bound - counts[i], max(1, budget * loads[i] // mass), spare)
            counts[i] = counts[i] + more
            spare = spare - more
    return np.array(counts)


def noise(key, extent, width, bound, cuts=(), kind=jnp.bfloat16):
    result = width * jax.random.normal(key, extent, jnp.float32)
    if cuts:
        result = result * level_of(key, extent, cuts, -0.22, 0.18)
    return jnp.clip(result, -bound, bound).astype(kind)


def setup_inputs(seed: int = 0) -> dict:
    splits = jax.random.split(jax.random.key(seed), 10)
    token_grads = noise(splits[0], (TOKENS, D), 1.0, 6.0, ((0, 192), (1, 4)))
    routes_keys = jax.random.split(jax.random.fold_in(splits[1], 1), TOKENS // TOK_DEV)
    routes_turns = jax.random.permutation(jax.random.fold_in(splits[1], 3), TOKENS // TOK_DEV)
    routes = jax.vmap(lambda own, number: deal_out(jax.random.fold_in(splits[1], 2), own, number, TOK_DEV, EXPERTS, TOP, CAP, 2))(routes_keys, routes_turns).reshape((TOKENS, TOP))
    gates = jnp.clip(0.19921875 + 0.80078125 * jax.random.uniform(splits[2], (TOKENS, TOP), jnp.float32) ** level_of(splits[2], (TOKENS, TOP), ((0, 192),), -0.2, 0.2), 0.19921875, 1.0).astype(jnp.bfloat16)
    expert_inputs = noise(splits[3], (N_REPLICA, EXPERTS, N_LOCAL, CAP, D), 1.0, 6.0, ((0, 48), (1, 4), (4, 4)))
    gate_pre = noise(splits[4], (N_REPLICA, EXPERTS, N_LOCAL, CAP, FF), 1.5, 8.0, ((0, 48), (1, 4)))
    up_pre = noise(splits[5], (N_REPLICA, EXPERTS, N_LOCAL, CAP, FF), 1.0, 6.0, ((0, 48), (1, 4)))
    w_gate = noise(splits[6], (EXPERTS, D, FF), D ** -0.5, 0.09375, ((0, 4), (1, 4)))
    w_up = noise(splits[7], (EXPERTS, D, FF), D ** -0.5, 0.09375, ((0, 4), (1, 4)))
    w_down = noise(splits[8], (EXPERTS, FF, D), FF ** -0.5, 0.1875, ((0, 4), (2, 4)))
    return dict(token_grads=token_grads, routes=routes, gates=gates, expert_inputs=expert_inputs, gate_pre=gate_pre, up_pre=up_pre, w_gate=w_gate, w_up=w_up, w_down=w_down)


def reference(token_grads, routes, gates, expert_inputs, gate_pre, up_pre, w_gate, w_up, w_down):
    blocks = N_REPLICA * N_LOCAL
    picks = routes.reshape(blocks, TOK_DEV * TOP).astype(jnp.int32)
    onehot = (picks[:, :, None] == jnp.arange(EXPERTS, dtype=jnp.int32)[None, None, :]).astype(jnp.int32)
    before = jnp.cumsum(onehot, axis=1) - onehot
    slot_of = jnp.sum(before * onehot, axis=2).astype(jnp.int32)
    target = (picks * CAP + slot_of).astype(jnp.int32)
    block_ids = jnp.arange(blocks, dtype=jnp.int32)[:, None]
    spread = jnp.repeat(token_grads.reshape(blocks, TOK_DEV, D), TOP, axis=1)
    sent = jnp.zeros((blocks, EXPERTS * CAP, D), token_grads.dtype).at[block_ids, target].set(spread)
    sent_gates = jnp.zeros((blocks, EXPERTS * CAP), jnp.float32).at[block_ids, target].set(
        gates.reshape(blocks, TOK_DEV * TOP).astype(jnp.float32))
    arrived = sent.reshape(N_REPLICA, N_LOCAL, EXPERTS, CAP, D).transpose(0, 2, 1, 3, 4)
    arrived_gates = sent_gates.reshape(N_REPLICA, N_LOCAL, EXPERTS, CAP).transpose(0, 2, 1, 3)
    gate_f = w_gate.astype(jnp.float32)
    up_f = w_up.astype(jnp.float32)
    down_f = w_down.astype(jnp.float32)

    def one_copy(carry, item):
        dy_rows, g_rows, x_rows, g_pre, u_pre = item
        dy_rows = dy_rows.reshape(EXPERTS, N_LOCAL * CAP, D).astype(jnp.float32)
        g_rows = g_rows.reshape(EXPERTS, N_LOCAL * CAP, 1)
        x_rows = x_rows.reshape(EXPERTS, N_LOCAL * CAP, D).astype(jnp.float32)
        gpre = g_pre.reshape(EXPERTS, N_LOCAL * CAP, FF).astype(jnp.float32)
        upre = u_pre.reshape(EXPERTS, N_LOCAL * CAP, FF).astype(jnp.float32)
        raw = jnp.einsum('esd,efd->esf', dy_rows, down_f)
        sig = jax.nn.sigmoid(gpre)
        act = gpre * sig
        dgate = jnp.sum(raw * act * upre, axis=2).astype(jnp.bfloat16)
        scaled = raw * g_rows
        gate_delta = (scaled * upre * sig * (1.0 + gpre * (1.0 - sig))).astype(jnp.bfloat16)
        up_delta = (scaled * act).astype(jnp.bfloat16)
        slot_input = (jnp.einsum('esf,edf->esd', gate_delta.astype(jnp.float32), gate_f)
                      + jnp.einsum('esf,edf->esd', up_delta.astype(jnp.float32), up_f)).astype(jnp.bfloat16)
        gate_sum = carry[0] + jnp.einsum('esd,esf->edf', x_rows, gate_delta.astype(jnp.float32))
        up_sum = carry[1] + jnp.einsum('esd,esf->edf', x_rows, up_delta.astype(jnp.float32))
        return (gate_sum, up_sum), (slot_input, dgate)

    start = (jnp.zeros((EXPERTS, D, FF), jnp.float32), jnp.zeros((EXPERTS, D, FF), jnp.float32))
    sums, outs = lax.scan(one_copy, start, (arrived, arrived_gates, expert_inputs, gate_pre, up_pre))
    slot_input, dgate = outs
    back = slot_input.reshape(N_REPLICA, EXPERTS, N_LOCAL, CAP, D).transpose(0, 2, 1, 3, 4)
    back = back.reshape(blocks, EXPERTS * CAP, D)
    back_gate = dgate.reshape(N_REPLICA, EXPERTS, N_LOCAL, CAP).transpose(0, 2, 1, 3).reshape(blocks, EXPERTS * CAP)
    taken = back[block_ids, target].astype(jnp.float32).reshape(blocks, TOK_DEV, TOP, D)
    input_grads = jnp.sum(taken, axis=2).astype(jnp.bfloat16).reshape(TOKENS, D)
    gate_grads = back_gate[block_ids, target].reshape(TOKENS, TOP).astype(jnp.bfloat16)
    flat_rows = (D // N_NODE) * FF // 128
    gate_weight_grads = (sums[0] / N_REPLICA).reshape(EXPERTS, N_NODE, flat_rows, 128)
    up_weight_grads = (sums[1] / N_REPLICA).reshape(EXPERTS, N_NODE, flat_rows, 128)
    return input_grads, gate_grads, gate_weight_grads, up_weight_grads
```

```python
import functools

import jax
import jax.numpy as jnp
from jax import lax
from jax.experimental import pallas as pl
from jax.experimental.pallas import tpu as pltpu
from jax.sharding import Mesh
from jax.sharding import PartitionSpec as P

BF = jnp.bfloat16
F32 = jnp.float32
MIB = 1 << 20


def picks_of(routes, n_local, capacity):
    tokens, top = routes.shape
    lanes = lax.broadcasted_iota(jnp.int32, (tokens, 128), 1)
    named = [(lanes == routes[:, k : k + 1]) for k in range(top)]
    total = sum(jnp.where(n, 1.0, 0.0) for n in named).astype(BF)
    rows = lax.broadcasted_iota(jnp.int32, (tokens, tokens), 0)
    cols = lax.broadcasted_iota(jnp.int32, (tokens, tokens), 1)
    earlier = jnp.where(cols < rows, 1.0, 0.0).astype(BF)
    before = jnp.dot(earlier, total, preferred_element_type=F32)
    slots = lax.broadcasted_iota(jnp.int32, (tokens, n_local * capacity), 1)
    masks = []
    for k in range(top):
        slot = jnp.sum(jnp.where(named[k], before, 0.0), axis=1, keepdims=True)
        masks.append(slots == routes[:, k : k + 1] * capacity + slot.astype(jnp.int32))
    return masks


def dispatch_kernel(n_local, capacity, routes_ref, gates_ref, rows_ref, out_ref):
    masks = picks_of(routes_ref[...], n_local, capacity)
    gates = gates_ref[...].astype(F32)
    scaled = sum(
        jnp.where(m, gates[:, k : k + 1], 0.0) for k, m in enumerate(masks)
    ).astype(BF)
    out = lax.dot_general(
        scaled, rows_ref[...], (((0,), (0,)), ((), ())), preferred_element_type=F32
    ).astype(BF)
    for e in range(n_local):
        out_ref[e] = out[e * capacity : (e + 1) * capacity]


def raw_kernel(rows_ref, down_ref, out_ref):
    out_ref[0] = lax.dot_general(
        rows_ref[...], down_ref[...], (((1,), (1,)), ((), ())), preferred_element_type=F32
    ).astype(BF)


def sum_kernel(parts_ref, out_ref):
    total = parts_ref[0].astype(F32)
    for i in range(1, parts_ref.shape[0]):
        total = total + parts_ref[i].astype(F32)
    out_ref[...] = total.astype(BF)


def delta_kernel(raw_ref, gate_ref, up_ref, x_ref, grad_ref, delta_ref, dgate_ref):
    step = pl.program_id(0)
    raw = raw_ref[0].astype(F32)
    g = gate_ref[...].astype(F32)
    u = up_ref[...].astype(F32)
    sig = 1.0 / (1.0 + jnp.exp(-g))
    act = g * sig
    up_delta = raw * act
    gate_delta = raw * u * sig * (1.0 + g * (1.0 - sig))
    both = jnp.concatenate([gate_delta.astype(BF), up_delta.astype(BF)], axis=1)
    delta_ref[0] = both
    grad_ref[...] = jnp.dot(x_ref[...], both, preferred_element_type=F32).astype(BF)

    @pl.when(step == 0)
    def _():
        dgate_ref[...] = jnp.zeros_like(dgate_ref)

    dgate_ref[...] += jnp.broadcast_to(
        jnp.sum(up_delta * u, axis=1, keepdims=True), dgate_ref.shape
    )


def input_kernel(feat, delta_ref, wg_ref, wu_ref, dgate_ref, out_ref, total):
    step = pl.program_id(0)
    quarter = wg_ref.shape[1]
    dims = (((1,), (1,)), ((), ()))
    term = lax.dot_general(
        delta_ref[0, :, :quarter], wg_ref[...], dims, preferred_element_type=F32
    ) + lax.dot_general(delta_ref[0, :, quarter:], wu_ref[...], dims, preferred_element_type=F32)

    @pl.when(step == 0)
    def _():
        total[...] = term

    @pl.when(step > 0)
    def _():
        total[...] += term

    @pl.when(step == pl.num_programs(0) - 1)
    def _():
        rest = out_ref.shape[1] - feat
        out_ref[:, :feat] = total[...].astype(BF)
        out_ref[:, feat:] = dgate_ref[:, :rest].astype(BF)


def combine_kernel(n_local, capacity, routes_ref, gates_ref, back_ref, rows_ref, grads_ref):
    masks = [jnp.where(m, 1.0, 0.0).astype(BF) for m in picks_of(routes_ref[...], n_local, capacity)]
    feat = rows_ref.shape[1]
    back = back_ref[...]
    rows_ref[...] = jnp.dot(
        sum(masks[1:], masks[0]), back[:, :feat], preferred_element_type=F32
    ).astype(BF)
    tail = back[:, back.shape[1] - 128 :]
    gates = gates_ref[...].astype(F32)
    for k, m in enumerate(masks):
        own = jnp.dot(m, tail, preferred_element_type=F32)[:, 127:128]
        grads_ref[:, k : k + 1] = (own / gates[:, k : k + 1]).astype(BF)


def params(mib=32, **more):
    return pltpu.CompilerParams(vmem_limit_bytes=mib * MIB, **more)


def local(token_grads, routes, gates, expert_inputs, gate_pre, up_pre, w_gate, w_up, w_down):
    tokens, top = routes.shape
    n_local = lax.axis_size("local")
    n_node = lax.axis_size("node")
    n_z = lax.axis_size("z")
    n_y = lax.axis_size("y")
    n_copies = n_y * n_z
    capacity = expert_inputs.shape[3]
    feat = token_grads.shape[1]
    hidden = gate_pre.shape[4]
    quarter = hidden // n_node
    slots = n_local * capacity
    own = feat // n_copies
    wide = -(-(feat + 1) // 128) * 128

    outgoing = pl.pallas_call(
        functools.partial(dispatch_kernel, n_local, capacity),
        out_shape=jax.ShapeDtypeStruct((n_local, capacity, feat), BF),
        compiler_params=params(),
        name="dispatch",
    )(routes, gates, token_grads)
    arrived = lax.all_to_all(outgoing, "local", split_axis=0, concat_axis=0, tiled=True)

    raw_parts = pl.pallas_call(
        raw_kernel,
        grid=(n_node,),
        in_specs=[
            pl.BlockSpec((slots, feat), lambda i: (0, 0)),
            pl.BlockSpec((quarter, feat), lambda i: (i, 0)),
        ],
        out_specs=pl.BlockSpec((1, slots, quarter), lambda i: (i, 0, 0)),
        out_shape=jax.ShapeDtypeStruct((n_node, slots, quarter), BF),
        compiler_params=params(),
        name="raw",
    )(arrived.reshape(slots, feat), w_down[0])
    raw_shares = lax.all_to_all(raw_parts, "node", split_axis=0, concat_axis=0, tiled=True)
    raw_share = pl.pallas_call(
        sum_kernel,
        out_shape=jax.ShapeDtypeStruct((slots, quarter), BF),
        compiler_params=params(),
        name="share",
    )(raw_shares)
    raw = lax.all_gather(raw_share, "node", axis=0, tiled=False)

    x_rows = (
        expert_inputs[0, 0]
        .reshape(slots, n_y, n_z, own)
        .transpose(2, 1, 3, 0)
        .reshape(feat, slots)
    )
    grad, delta, dgate = pl.pallas_call(
        delta_kernel,
        grid=(n_node,),
        in_specs=[
            pl.BlockSpec((1, slots, quarter), lambda i: (i, 0, 0)),
            pl.BlockSpec((slots, quarter), lambda i: (0, i)),
            pl.BlockSpec((slots, quarter), lambda i: (0, i)),
            pl.BlockSpec((feat, slots), lambda i: (0, 0)),
        ],
        out_specs=[
            pl.BlockSpec((feat, 2 * quarter), lambda i: (0, i)),
            pl.BlockSpec((1, slots, 2 * quarter), lambda i: (i, 0, 0)),
            pl.BlockSpec((slots, 128), lambda i: (0, 0)),
        ],
        out_shape=[
            jax.ShapeDtypeStruct((feat, 2 * hidden), BF),
            jax.ShapeDtypeStruct((n_node, slots, 2 * quarter), BF),
            jax.ShapeDtypeStruct((slots, 128), F32),
        ],
        compiler_params=params(),
        name="delta",
    )(raw, gate_pre.reshape(slots, hidden), up_pre.reshape(slots, hidden), x_rows)

    z_sum = lax.psum_scatter(grad, "z", scatter_dimension=0, tiled=True)

    slot_input = pl.pallas_call(
        functools.partial(input_kernel, feat),
        grid=(n_node,),
        in_specs=[
            pl.BlockSpec((1, slots, 2 * quarter), lambda i: (i, 0, 0)),
            pl.BlockSpec((feat, quarter), lambda i: (0, i)),
            pl.BlockSpec((feat, quarter), lambda i: (0, i)),
            pl.BlockSpec((slots, 128), lambda i: (0, 0)),
        ],
        out_specs=pl.BlockSpec((slots, wide), lambda i: (0, 0)),
        out_shape=jax.ShapeDtypeStruct((slots, wide), BF),
        scratch_shapes=[pltpu.VMEM((slots, feat), F32)],
        compiler_params=params(),
        name="slot_input",
    )(delta, w_gate[0], w_up[0], dgate)
    back = lax.all_to_all(
        slot_input.reshape(n_local, capacity, wide), "local", split_axis=0, concat_axis=0, tiled=True
    )
    input_grads, gate_grads = pl.pallas_call(
        functools.partial(combine_kernel, n_local, capacity),
        out_shape=[
            jax.ShapeDtypeStruct((tokens, feat), BF),
            jax.ShapeDtypeStruct((tokens, top), BF),
        ],
        compiler_params=params(),
        name="combine",
    )(routes, gates, back.reshape(slots, wide))

    y_parts = lax.all_to_all(
        z_sum.reshape(n_y, own, 2 * hidden), "y", split_axis=0, concat_axis=0, tiled=True
    )
    total = jnp.sum(y_parts.astype(F32), axis=0) / n_copies
    total = total.reshape(own, n_node, 2, quarter)
    rows = own * hidden // 128
    gate_weight_grads = total[:, :, 0].reshape(1, 1, rows, 128)
    up_weight_grads = total[:, :, 1].reshape(1, 1, rows, 128)
    return (input_grads, gate_grads, gate_weight_grads, up_weight_grads)


def solution(mesh):
    n_y = 4
    shape = mesh.devices.shape
    cut = Mesh(
        mesh.devices.reshape(n_y, shape[0] // n_y, shape[1], shape[2]), ("y", "z", "node", "local")
    )
    replica = ("y", "z")
    placed = (
        P((*replica, "local"), "node"),
        P((*replica, "local"), None),
        P((*replica, "local"), None),
        P(replica, "local", None, None, "node"),
        P(replica, "local", None, None, None),
        P(replica, "local", None, None, None),
        P("local", "node", None),
        P("local", "node", None),
        P("local", None, "node"),
    )
    return jax.shard_map(
        local,
        mesh=cut,
        in_specs=placed,
        out_specs=(
            P((*replica, "local"), "node"),
            P((*replica, "local"), None),
            P("local", "node", replica, None),
            P("local", "node", replica, None),
        ),
        check_vma=False,
    )
```

```python
import functools

import jax
import jax.numpy as jnp
from jax import lax
from jax.experimental import pallas as pl
from jax.experimental.pallas import tpu as pltpu
from jax.sharding import Mesh
from jax.sharding import PartitionSpec as P

BF = jnp.bfloat16
F32 = jnp.float32
MIB = 1 << 20


CUT = (4, 3, 4)


def picks_of(routes, n_local, capacity, turn=None):
    tokens, top = routes.shape
    lanes = lax.broadcasted_iota(jnp.int32, (tokens, 128), 1)
    named = [(lanes == routes[:, k : k + 1]) for k in range(top)]
    total = sum(jnp.where(n, 1.0, 0.0) for n in named).astype(BF)
    rows = lax.broadcasted_iota(jnp.int32, (tokens, tokens), 0)
    cols = lax.broadcasted_iota(jnp.int32, (tokens, tokens), 1)
    earlier = jnp.where(cols < rows, 1.0, 0.0).astype(BF)
    before = jnp.dot(earlier, total, preferred_element_type=F32)
    slots = lax.broadcasted_iota(jnp.int32, (tokens, n_local * capacity), 1)
    block = routes if turn is None else jnp.bitwise_xor(routes, turn)
    masks = []
    for k in range(top):
        slot = jnp.sum(jnp.where(named[k], before, 0.0), axis=1, keepdims=True)
        masks.append(slots == block[:, k : k + 1] * capacity + slot.astype(jnp.int32))
    return masks


def dispatch_kernel(n_local, capacity, routes_ref, gates_ref, rows_ref, out_ref):
    masks = picks_of(routes_ref[...].T, n_local, capacity)
    gates = gates_ref[...].astype(F32).T
    scaled = sum(jnp.where(m, gates[:, k : k + 1], 0.0) for k, m in enumerate(masks)).astype(BF)
    out = lax.dot_general(
        scaled, rows_ref[...], (((0,), (1,)), ((), ())), preferred_element_type=F32
    ).astype(BF)
    for e in range(n_local):
        out_ref[e] = out[e * capacity : (e + 1) * capacity]


def raw_kernel(rows_ref, down_ref, out_ref):
    out_ref[0] = jnp.dot(rows_ref[...], down_ref[...], preferred_element_type=F32).astype(BF)


def sum_kernel(parts_ref, out_ref):
    total = parts_ref[0].astype(F32)
    for i in range(1, parts_ref.shape[0]):
        total = total + parts_ref[i].astype(F32)
    out_ref[...] = total.astype(BF)


def factors(g, u):
    sig = 1.0 / (1.0 + jnp.exp(-g))
    return u * sig * (1.0 + g * (1.0 - sig)), g * sig


def early_kernel(own, n_zl, place_ref, x_ref, gate_ref, up_ref, slab_ref, fact_ref):
    zl, node = place_ref[0], place_ref[1]
    feat = x_ref.shape[1]
    part = feat // n_zl
    quarter = fact_ref.shape[1] // 2
    at = lax.broadcasted_iota(jnp.int32, (part, 1), 0)
    group = jnp.floor((at.astype(F32) + 0.5) * (1.0 / own)).astype(jnp.int32)
    cols = lax.broadcasted_iota(jnp.int32, (part, feat), 1)
    x = x_ref[...]
    for k in range(n_zl):
        to = jnp.bitwise_and(zl + k, n_zl - 1)
        wanted = (group * n_zl + to) * own + (at - group * own)
        chosen = jnp.where(cols == wanted, 1.0, 0.0).astype(BF)
        slab_ref[k] = lax.dot_general(
            chosen, x, (((1,), (1,)), ((), ())), preferred_element_type=F32
        ).astype(BF)
    here = pl.ds(pl.multiple_of(node * quarter, quarter), quarter)
    for_gate, for_up = factors(gate_ref[:, here].astype(F32), up_ref[:, here].astype(F32))
    fact_ref[:, :quarter] = for_gate.astype(BF)
    fact_ref[:, quarter:] = for_up.astype(BF)


def grads_kernel(own, place_ref, raw_ref, fact_ref, *rest):
    x_refs, (out_ref, keep_ref, delta) = rest[:-3], rest[-3:]
    zl, node = place_ref[0], place_ref[1]
    n_zl, slots, quarter = raw_ref.shape
    for k in range(n_zl):
        copy = jnp.bitwise_and(zl + n_zl - k, n_zl - 1)
        raw = raw_ref[copy].astype(F32)
        fact = fact_ref[copy].astype(F32)
        if k == 0:
            keep_ref[...] = raw_ref[copy]
        rows = slice(k * slots, (k + 1) * slots)
        delta[rows, :quarter] = (raw * fact[:, :quarter]).astype(BF)
        delta[rows, quarter:] = (raw * fact[:, quarter:]).astype(BF)
    d = delta[...]
    n_node = len(x_refs)
    for k in range(n_node):
        block = jnp.bitwise_and(node + n_node - k, n_node - 1)
        res = jnp.dot(x_refs[k][...], d, preferred_element_type=F32)
        for i in range(out_ref.shape[0]):
            piece = res[i * own : (i + 1) * own]
            tall = jnp.concatenate(
                [piece[:, c * 128 : (c + 1) * 128] for c in range(piece.shape[1] // 128)], axis=0
            )
            out_ref[i, block] = tall.astype(BF)


def input_kernel(capacity, place_ref, raw_ref, gate_ref, up_ref, wg_ref, wu_ref, out_ref, total, side):
    step = pl.program_id(0)
    raw = raw_ref[0].astype(F32)
    u = up_ref[...].astype(F32)
    for_gate, for_up = factors(gate_ref[...].astype(F32), u)
    up_delta = raw * for_up
    dims = (((1,), (1,)), ((), ()))
    term = lax.dot_general(
        (raw * for_gate).astype(BF), wg_ref[...], dims, preferred_element_type=F32
    ) + lax.dot_general(up_delta.astype(BF), wu_ref[...], dims, preferred_element_type=F32)
    dgate = jnp.broadcast_to(jnp.sum(up_delta * u, axis=1, keepdims=True), side.shape)

    @pl.when(step == 0)
    def _():
        total[...] = term
        side[...] = dgate

    @pl.when(step > 0)
    def _():
        total[...] += term
        side[...] += dgate

    @pl.when(step == pl.num_programs(0) - 1)
    def _():
        feat = total.shape[1]
        rest = out_ref.shape[2] - feat
        for k in range(out_ref.shape[0]):
            to = jnp.bitwise_xor(place_ref[2], k)
            rows = pl.ds(pl.multiple_of(to * capacity, 8), capacity)
            out_ref[k, :, :feat] = total[rows, :].astype(BF)
            out_ref[k, :, feat:] = side[rows, :rest].astype(BF)


def combine_kernel(n_local, capacity, place_ref, routes_ref, gates_ref, *rest):
    back_refs, (rows_ref, grads_ref) = rest[:-2], rest[-2:]
    masks = [
        jnp.where(m, 1.0, 0.0).astype(BF)
        for m in picks_of(routes_ref[...].T, n_local, capacity, place_ref[2])
    ]
    feat = rows_ref.shape[0]
    back = jnp.concatenate([r[...] for r in back_refs], axis=0)
    rows_ref[...] = lax.dot_general(
        back[:, :feat], sum(masks[1:], masks[0]), (((0,), (1,)), ((), ())), preferred_element_type=F32
    ).astype(BF)
    tail = back[:, back.shape[1] - 128 :]
    gates = gates_ref[...].astype(F32)
    for k, m in enumerate(masks):
        sums = lax.dot_general(
            tail, m, (((0,), (1,)), ((), ())), preferred_element_type=F32
        )[127:128]
        grads_ref[k : k + 1, :] = (sums / gates[k : k + 1, :]).astype(BF)


def final_kernel(n_copies, own, parts_ref, gate_ref, up_ref):
    copies, n_node = parts_ref.shape[0], parts_ref.shape[1]
    for x in range(n_node):
        total = parts_ref[0, x].astype(F32)
        for i in range(1, copies):
            total = total + parts_ref[i, x].astype(F32)
        total = total * (1.0 / n_copies)
        per = total.shape[0] // own // 2
        for c in range(2 * per):
            out = gate_ref if c < per else up_ref
            out[:, x * per + c % per, :] = total[c * own : (c + 1) * own]


def params(mib=32, **more):
    return pltpu.CompilerParams(vmem_limit_bytes=mib * MIB, **more)


def ring(x, axis, step):
    n = lax.axis_size(axis)
    return lax.ppermute(x, axis, [(i, (i + step) % n) for i in range(n)])


SMEM = pl.BlockSpec(memory_space=pltpu.SMEM)
VMEM = pl.BlockSpec(memory_space=pltpu.VMEM)


def local(token_grads, routes, gates, expert_inputs, gate_pre, up_pre, w_gate, w_up, w_down):
    tokens, top = routes.shape
    n_local = lax.axis_size("local")
    n_node = lax.axis_size("node")
    n_zl, n_zh, n_y = lax.axis_size("zl"), lax.axis_size("zh"), lax.axis_size("y")
    n_copies = n_y * n_zh * n_zl
    capacity = expert_inputs.shape[3]
    feat = token_grads.shape[1]
    hidden = gate_pre.shape[4]
    quarter = hidden // n_node
    slots = n_local * capacity
    own = feat // n_copies
    part = feat // n_zl
    wide = -(-(feat + 1) // 128) * 128
    place = jnp.stack([lax.axis_index(a) for a in ("zl", "node", "local")]).astype(jnp.int32)
    gate_rows = gate_pre.reshape(slots, hidden)
    up_rows = up_pre.reshape(slots, hidden)
    x_rows = expert_inputs.reshape(slots, feat)

    outgoing = pl.pallas_call(
        functools.partial(dispatch_kernel, n_local, capacity),
        out_shape=jax.ShapeDtypeStruct((n_local, capacity, feat), BF),
        compiler_params=params(),
        name="dispatch",
    )(routes.T, gates.T, token_grads.T)
    arrived = lax.all_to_all(outgoing, "local", split_axis=0, concat_axis=0, tiled=True)

    x_rows, _ = lax.optimization_barrier((x_rows, outgoing))
    slabs, facts = pl.pallas_call(
        functools.partial(early_kernel, own, n_zl),
        in_specs=[SMEM, VMEM, VMEM, VMEM],
        out_shape=[
            jax.ShapeDtypeStruct((n_zl, part, slots), BF),
            jax.ShapeDtypeStruct((slots, 2 * quarter), BF),
        ],
        compiler_params=params(),
        name="early",
    )(place, x_rows, gate_rows, up_rows)
    all_facts = lax.all_gather(facts, "zl", axis=0, tiled=False)
    copies_x = [slabs[0]] + [ring(slabs[k], "zl", k) for k in range(1, n_zl)]

    raw_parts = pl.pallas_call(
        raw_kernel,
        grid=(n_node,),
        in_specs=[
            pl.BlockSpec((slots, feat), lambda i: (0, 0)),
            pl.BlockSpec((feat, quarter), lambda i: (0, i)),
        ],
        out_specs=pl.BlockSpec((1, slots, quarter), lambda i: (i, 0, 0)),
        out_shape=jax.ShapeDtypeStruct((n_node, slots, quarter), BF),
        compiler_params=params(),
        name="raw",
    )(arrived.reshape(slots, feat), w_down[0].T)
    raw_shares = lax.all_to_all(raw_parts, "node", split_axis=0, concat_axis=0, tiled=True)

    *copies_x, _ = lax.optimization_barrier((*copies_x, raw_parts))
    own_x = jnp.concatenate(copies_x, axis=1)
    node_x = [own_x] + [ring(own_x, "node", k) for k in range(1, n_node)]

    raw_share = pl.pallas_call(
        sum_kernel,
        out_shape=jax.ShapeDtypeStruct((slots, quarter), BF),
        compiler_params=params(),
        name="share",
    )(raw_shares)
    raw_copies = lax.all_gather(raw_share, "zl", axis=0, tiled=False)

    tall = own * 2 * quarter // 128
    grads, kept = pl.pallas_call(
        functools.partial(grads_kernel, own),
        in_specs=[SMEM] + [VMEM] * (2 + n_node),
        out_shape=[
            jax.ShapeDtypeStruct((n_y * n_zh, n_node, tall, 128), BF),
            jax.ShapeDtypeStruct((slots, quarter), BF),
        ],
        scratch_shapes=[pltpu.VMEM((n_zl * slots, 2 * quarter), BF)],
        compiler_params=params(),
        name="grads",
    )(place, raw_copies, all_facts, *node_x)
    parts = lax.all_to_all(
        grads.reshape(n_y * n_zh * n_node, tall, 128),
        ("y", "zh", "node"),
        split_axis=0,
        concat_axis=0,
        tiled=True,
    )

    raw = lax.all_gather(kept, "node", axis=0, tiled=False)
    slot_input = pl.pallas_call(
        functools.partial(input_kernel, capacity),
        grid=(n_node,),
        in_specs=[
            SMEM,
            pl.BlockSpec((1, slots, quarter), lambda i: (i, 0, 0)),
            pl.BlockSpec((slots, quarter), lambda i: (0, i)),
            pl.BlockSpec((slots, quarter), lambda i: (0, i)),
            pl.BlockSpec((feat, quarter), lambda i: (0, i)),
            pl.BlockSpec((feat, quarter), lambda i: (0, i)),
        ],
        out_specs=pl.BlockSpec((n_local, capacity, wide), lambda i: (0, 0, 0)),
        out_shape=jax.ShapeDtypeStruct((n_local, capacity, wide), BF),
        scratch_shapes=[pltpu.VMEM((slots, feat), F32), pltpu.VMEM((slots, 128), F32)],
        compiler_params=params(),
        name="slot_input",
    )(place, raw, gate_rows, up_rows, w_gate[0], w_up[0])
    back = [slot_input[0]] + [
        lax.ppermute(slot_input[k], "local", [(i, i ^ k) for i in range(n_local)])
        for k in range(1, n_local)
    ]
    input_grads, gate_grads = pl.pallas_call(
        functools.partial(combine_kernel, n_local, capacity),
        in_specs=[SMEM] + [VMEM] * (2 + n_local),
        out_shape=[
            jax.ShapeDtypeStruct((feat, tokens), BF),
            jax.ShapeDtypeStruct((top, tokens), BF),
        ],
        compiler_params=params(),
        name="combine",
    )(place, routes.T, gates.T, *back)

    gate_sum, up_sum = pl.pallas_call(
        functools.partial(final_kernel, n_copies, own),
        out_shape=[jax.ShapeDtypeStruct((own, hidden // 128, 128), F32)] * 2,
        compiler_params=params(),
        name="final",
    )(parts.reshape(n_y * n_zh, n_node, tall, 128))
    rows = own * hidden // 128
    return (
        input_grads.T,
        gate_grads.T,
        gate_sum.reshape(1, 1, rows, 128),
        up_sum.reshape(1, 1, rows, 128),
    )


def solution(mesh):
    shape = mesh.devices.shape
    cut = Mesh(mesh.devices.reshape(*CUT, shape[1], shape[2]), ("y", "zh", "zl", "node", "local"))
    replica = ("y", "zh", "zl")
    placed = (
        P((*replica, "local"), "node"),
        P((*replica, "local"), None),
        P((*replica, "local"), None),
        P(replica, "local", None, None, "node"),
        P(replica, "local", None, None, None),
        P(replica, "local", None, None, None),
        P("local", "node", None),
        P("local", "node", None),
        P("local", None, "node"),
    )
    return jax.shard_map(
        local,
        mesh=cut,
        in_specs=placed,
        out_specs=(
            P((*replica, "local"), "node"),
            P((*replica, "local"), None),
            P("local", "node", replica, None),
            P("local", "node", replica, None),
        ),
        check_vma=False,
    )
```

```python
import functools

import jax
import jax.numpy as jnp
from jax import lax
from jax.experimental import pallas as pl
from jax.experimental.pallas import tpu as pltpu
from jax.sharding import Mesh
from jax.sharding import PartitionSpec as P

BF = jnp.bfloat16
F32 = jnp.float32
MIB = 1 << 20


CUT = (4, 3, 4)


def picks_of(routes, n_local, capacity, turn=None):
    tokens, top = routes.shape
    lanes = lax.broadcasted_iota(jnp.int32, (tokens, 128), 1)
    named = [(lanes == routes[:, k : k + 1]) for k in range(top)]
    total = sum(jnp.where(n, 1.0, 0.0) for n in named).astype(BF)
    rows = lax.broadcasted_iota(jnp.int32, (tokens, tokens), 0)
    cols = lax.broadcasted_iota(jnp.int32, (tokens, tokens), 1)
    earlier = jnp.where(cols < rows, 1.0, 0.0).astype(BF)
    before = jnp.dot(earlier, total, preferred_element_type=F32)
    slots = lax.broadcasted_iota(jnp.int32, (tokens, n_local * capacity), 1)
    block = routes if turn is None else jnp.bitwise_xor(routes, turn)
    masks = []
    for k in range(top):
        slot = jnp.sum(jnp.where(named[k], before, 0.0), axis=1, keepdims=True)
        masks.append(slots == block[:, k : k + 1] * capacity + slot.astype(jnp.int32))
    return masks


def dispatch_kernel(n_local, capacity, routes_ref, gates_ref, rows_ref, out_ref):
    masks = picks_of(routes_ref[...].T, n_local, capacity)
    gates = gates_ref[...].astype(F32).T
    scaled = sum(jnp.where(m, gates[:, k : k + 1], 0.0) for k, m in enumerate(masks)).astype(BF)
    out = lax.dot_general(
        scaled, rows_ref[...], (((0,), (1,)), ((), ())), preferred_element_type=F32
    ).astype(BF)
    for e in range(n_local):
        out_ref[e] = out[e * capacity : (e + 1) * capacity]


def raw_kernel(rows_ref, down_ref, out_ref):
    out_ref[0] = jnp.dot(rows_ref[...], down_ref[...], preferred_element_type=F32).astype(BF)


def factors(g, u):
    sig = 1.0 / (1.0 + jnp.exp(-g))
    return u * sig * (1.0 + g * (1.0 - sig)), g * sig


def early_kernel(n_y, place_ref, x_ref, out_ref):
    y = place_ref[0]
    feat = x_ref.shape[1]
    part = feat // n_y
    at = lax.broadcasted_iota(jnp.int32, (part, feat), 1) - lax.broadcasted_iota(
        jnp.int32, (part, feat), 0
    )
    x = x_ref[...]
    for k in range(n_y):
        first = jnp.bitwise_and(y + k, n_y - 1) * part
        chosen = jnp.where(at == first, 1.0, 0.0).astype(BF)
        out_ref[k] = lax.dot_general(
            chosen, x, (((1,), (1,)), ((), ())), preferred_element_type=F32
        ).astype(BF)


def share_kernel(place_ref, parts_ref, gate_ref, up_ref, raw_ref, delta_ref):
    quarter = raw_ref.shape[1]
    raw = parts_ref[0].astype(F32)
    for i in range(1, parts_ref.shape[0]):
        raw = raw + parts_ref[i].astype(F32)
    raw_ref[...] = raw.astype(BF)
    here = pl.ds(pl.multiple_of(place_ref[1] * quarter, quarter), quarter)
    for_gate, for_up = factors(gate_ref[:, here].astype(F32), up_ref[:, here].astype(F32))
    gate_delta = (raw * for_gate).astype(BF)
    up_delta = (raw * for_up).astype(BF)
    for k in range(delta_ref.shape[0]):
        delta_ref[k, :, :quarter] = gate_delta
        delta_ref[k, :, quarter:] = up_delta


def grads_kernel(own, place_ref, delta_ref, x_ref, out_ref, ordered):
    n_y, slots, _ = delta_ref.shape
    for k in range(n_y):
        copy = jnp.bitwise_and(place_ref[0] + n_y - k, n_y - 1)
        ordered[k * slots : (k + 1) * slots] = delta_ref[copy]
    d = ordered[...]
    n_zl, n_zh, n_node = out_ref.shape[:3]
    for b in range(n_node):
        res = jnp.dot(x_ref[b], d, preferred_element_type=F32)
        for i in range(n_zh * n_zl):
            piece = res[i * own : (i + 1) * own]
            tall = jnp.concatenate(
                [piece[:, c * 128 : (c + 1) * 128] for c in range(piece.shape[1] // 128)], axis=0
            )
            out_ref[i % n_zl, i // n_zl, b] = tall.astype(BF)


def sum_kernel(parts_ref, out_ref):
    total = parts_ref[0].astype(F32)
    for i in range(1, parts_ref.shape[0]):
        total = total + parts_ref[i].astype(F32)
    out_ref[...] = total.astype(BF)


def input_kernel(capacity, place_ref, raw_ref, gate_ref, up_ref, wg_ref, wu_ref, out_ref, total, side):
    step = pl.program_id(0)
    raw = raw_ref[0].astype(F32)
    u = up_ref[...].astype(F32)
    for_gate, for_up = factors(gate_ref[...].astype(F32), u)
    up_delta = raw * for_up
    dims = (((1,), (1,)), ((), ()))
    term = lax.dot_general(
        (raw * for_gate).astype(BF), wg_ref[...], dims, preferred_element_type=F32
    ) + lax.dot_general(up_delta.astype(BF), wu_ref[...], dims, preferred_element_type=F32)
    dgate = jnp.broadcast_to(jnp.sum(up_delta * u, axis=1, keepdims=True), side.shape)

    @pl.when(step == 0)
    def _():
        total[...] = term
        side[...] = dgate

    @pl.when(step > 0)
    def _():
        total[...] += term
        side[...] += dgate

    @pl.when(step == pl.num_programs(0) - 1)
    def _():
        feat = total.shape[1]
        rest = out_ref.shape[2] - feat
        for k in range(out_ref.shape[0]):
            to = jnp.bitwise_xor(place_ref[2], k)
            rows = pl.ds(pl.multiple_of(to * capacity, 8), capacity)
            out_ref[k, :, :feat] = total[rows, :].astype(BF)
            out_ref[k, :, feat:] = side[rows, :rest].astype(BF)


def combine_kernel(n_local, capacity, place_ref, routes_ref, gates_ref, *rest):
    back_refs, (rows_ref, grads_ref) = rest[:-2], rest[-2:]
    masks = [
        jnp.where(m, 1.0, 0.0).astype(BF)
        for m in picks_of(routes_ref[...].T, n_local, capacity, place_ref[2])
    ]
    feat = rows_ref.shape[0]
    back = jnp.concatenate([r[...] for r in back_refs], axis=0)
    rows_ref[...] = lax.dot_general(
        back[:, :feat], sum(masks[1:], masks[0]), (((0,), (1,)), ((), ())), preferred_element_type=F32
    ).astype(BF)
    tail = back[:, back.shape[1] - 128 :]
    gates = gates_ref[...].astype(F32)
    for k, m in enumerate(masks):
        sums = lax.dot_general(
            tail, m, (((0,), (1,)), ((), ())), preferred_element_type=F32
        )[127:128]
        grads_ref[k : k + 1, :] = (sums / gates[k : k + 1, :]).astype(BF)


def final_kernel(n_copies, own, parts_ref, gate_ref, up_ref):
    copies, n_node = parts_ref.shape[0], parts_ref.shape[1]
    for x in range(n_node):
        total = parts_ref[0, x].astype(F32)
        for i in range(1, copies):
            total = total + parts_ref[i, x].astype(F32)
        total = total * (1.0 / n_copies)
        per = total.shape[0] // own // 2
        for c in range(2 * per):
            out = gate_ref if c < per else up_ref
            out[:, x * per + c % per, :] = total[c * own : (c + 1) * own]


def params(mib=32, **more):
    return pltpu.CompilerParams(vmem_limit_bytes=mib * MIB, **more)


def ring(x, axis, step):
    n = lax.axis_size(axis)
    return lax.ppermute(x, axis, [(i, (i + step) % n) for i in range(n)])


SMEM = pl.BlockSpec(memory_space=pltpu.SMEM)
VMEM = pl.BlockSpec(memory_space=pltpu.VMEM)


def local(token_grads, routes, gates, expert_inputs, gate_pre, up_pre, w_gate, w_up, w_down):
    tokens, top = routes.shape
    n_local = lax.axis_size("local")
    n_node = lax.axis_size("node")
    n_zl, n_zh, n_y = lax.axis_size("zl"), lax.axis_size("zh"), lax.axis_size("y")
    n_copies = n_y * n_zh * n_zl
    capacity = expert_inputs.shape[3]
    feat = token_grads.shape[1]
    hidden = gate_pre.shape[4]
    quarter = hidden // n_node
    slots = n_local * capacity
    own = feat // n_copies
    part = feat // n_y
    wide = -(-(feat + 1) // 128) * 128
    place = jnp.stack([lax.axis_index(a) for a in ("y", "node", "local")]).astype(jnp.int32)
    gate_rows = gate_pre.reshape(slots, hidden)
    up_rows = up_pre.reshape(slots, hidden)
    x_rows = expert_inputs.reshape(slots, feat)

    outgoing = pl.pallas_call(
        functools.partial(dispatch_kernel, n_local, capacity),
        out_shape=jax.ShapeDtypeStruct((n_local, capacity, feat), BF),
        compiler_params=params(),
        name="dispatch",
    )(routes.T, gates.T, token_grads.T)
    arrived = lax.all_to_all(outgoing, "local", split_axis=0, concat_axis=0, tiled=True)

    x_rows, _ = lax.optimization_barrier((x_rows, outgoing))
    slabs = pl.pallas_call(
        functools.partial(early_kernel, n_y),
        in_specs=[SMEM, VMEM],
        out_shape=jax.ShapeDtypeStruct((n_y, part, slots), BF),
        compiler_params=params(),
        name="early",
    )(place, x_rows)
    copies_x = [slabs[0]] + [ring(slabs[k], "y", k) for k in range(1, n_y)]

    raw_parts = pl.pallas_call(
        raw_kernel,
        grid=(n_node,),
        in_specs=[
            pl.BlockSpec((slots, feat), lambda i: (0, 0)),
            pl.BlockSpec((feat, quarter), lambda i: (0, i)),
        ],
        out_specs=pl.BlockSpec((1, slots, quarter), lambda i: (i, 0, 0)),
        out_shape=jax.ShapeDtypeStruct((n_node, slots, quarter), BF),
        compiler_params=params(),
        name="raw",
    )(arrived.reshape(slots, feat), w_down[0].T)
    raw_shares = lax.all_to_all(raw_parts, "node", split_axis=0, concat_axis=0, tiled=True)

    *copies_x, raw_shares = lax.optimization_barrier((*copies_x, raw_shares))
    node_x = lax.all_gather(jnp.concatenate(copies_x, axis=1), "node", axis=0, tiled=False)

    raw_share, deltas = pl.pallas_call(
        share_kernel,
        in_specs=[SMEM, VMEM, VMEM, VMEM],
        out_shape=[
            jax.ShapeDtypeStruct((slots, quarter), BF),
            jax.ShapeDtypeStruct((n_y, slots, 2 * quarter), BF),
        ],
        compiler_params=params(),
        name="share",
    )(place, raw_shares, gate_rows, up_rows)
    all_deltas = lax.all_to_all(deltas, "y", split_axis=0, concat_axis=0, tiled=True)

    raw = lax.all_gather(raw_share, "node", axis=0, tiled=False)
    slot_input = pl.pallas_call(
        functools.partial(input_kernel, capacity),
        grid=(n_node,),
        in_specs=[
            SMEM,
            pl.BlockSpec((1, slots, quarter), lambda i: (i, 0, 0)),
            pl.BlockSpec((slots, quarter), lambda i: (0, i)),
            pl.BlockSpec((slots, quarter), lambda i: (0, i)),
            pl.BlockSpec((feat, quarter), lambda i: (0, i)),
            pl.BlockSpec((feat, quarter), lambda i: (0, i)),
        ],
        out_specs=pl.BlockSpec((n_local, capacity, wide), lambda i: (0, 0, 0)),
        out_shape=jax.ShapeDtypeStruct((n_local, capacity, wide), BF),
        scratch_shapes=[pltpu.VMEM((slots, feat), F32), pltpu.VMEM((slots, 128), F32)],
        compiler_params=params(),
        name="slot_input",
    )(place, raw, gate_rows, up_rows, w_gate[0], w_up[0])
    all_deltas, slot_input = lax.optimization_barrier((all_deltas, slot_input))

    tall = own * 2 * quarter // 128
    grads = pl.pallas_call(
        functools.partial(grads_kernel, own),
        in_specs=[SMEM, VMEM, VMEM],
        out_shape=jax.ShapeDtypeStruct((n_zl, n_zh, n_node, tall, 128), BF),
        scratch_shapes=[pltpu.VMEM((n_y * slots, 2 * quarter), BF)],
        compiler_params=params(),
        name="grads",
    )(place, all_deltas, node_x)
    near = lax.all_to_all(grads, "zl", split_axis=0, concat_axis=0, tiled=True)
    back = [slot_input[0]] + [
        lax.ppermute(slot_input[k], "local", [(i, i ^ k) for i in range(n_local)])
        for k in range(1, n_local)
    ]
    input_grads, gate_grads = pl.pallas_call(
        functools.partial(combine_kernel, n_local, capacity),
        in_specs=[SMEM] + [VMEM] * (2 + n_local),
        out_shape=[
            jax.ShapeDtypeStruct((feat, tokens), BF),
            jax.ShapeDtypeStruct((top, tokens), BF),
        ],
        compiler_params=params(),
        name="combine",
    )(place, routes.T, gates.T, *back)

    near, input_grads, gate_grads = lax.optimization_barrier((near, input_grads, gate_grads))
    near_sum = pl.pallas_call(
        sum_kernel,
        out_shape=jax.ShapeDtypeStruct((n_zh, n_node, tall, 128), BF),
        compiler_params=params(),
        name="near_sum",
    )(near)
    parts = lax.all_to_all(
        near_sum.reshape(n_zh * n_node, tall, 128),
        ("zh", "node"),
        split_axis=0,
        concat_axis=0,
        tiled=True,
    )

    gate_sum, up_sum = pl.pallas_call(
        functools.partial(final_kernel, n_copies, own),
        out_shape=[jax.ShapeDtypeStruct((own, hidden // 128, 128), F32)] * 2,
        compiler_params=params(),
        name="final",
    )(parts.reshape(n_zh, n_node, tall, 128))
    rows = own * hidden // 128
    return (
        input_grads.T,
        gate_grads.T,
        gate_sum.reshape(1, 1, rows, 128),
        up_sum.reshape(1, 1, rows, 128),
    )


def solution(mesh):
    shape = mesh.devices.shape
    cut = Mesh(mesh.devices.reshape(*CUT, shape[1], shape[2]), ("y", "zh", "zl", "node", "local"))
    replica = ("y", "zh", "zl")
    placed = (
        P((*replica, "local"), "node"),
        P((*replica, "local"), None),
        P((*replica, "local"), None),
        P(replica, "local", None, None, "node"),
        P(replica, "local", None, None, None),
        P(replica, "local", None, None, None),
        P("local", "node", None),
        P("local", "node", None),
        P("local", None, "node"),
    )
    return jax.shard_map(
        local,
        mesh=cut,
        in_specs=placed,
        out_specs=(
            P((*replica, "local"), "node"),
            P((*replica, "local"), None),
            P("local", "node", replica, None),
            P("local", "node", replica, None),
        ),
        check_vma=False,
    )
```

```python
import functools

import jax
import jax.numpy as jnp
from jax import lax
from jax.experimental import pallas as pl
from jax.experimental.pallas import tpu as pltpu
from jax.sharding import Mesh
from jax.sharding import PartitionSpec as P

BF = jnp.bfloat16
F32 = jnp.float32
MIB = 1 << 20


CUT = (4, 12)


def picks_of(routes, n_local, capacity, turn=None):
    tokens, top = routes.shape
    lanes = lax.broadcasted_iota(jnp.int32, (tokens, 128), 1)
    named = [(lanes == routes[:, k : k + 1]) for k in range(top)]
    total = sum(jnp.where(n, 1.0, 0.0) for n in named).astype(BF)
    rows = lax.broadcasted_iota(jnp.int32, (tokens, tokens), 0)
    cols = lax.broadcasted_iota(jnp.int32, (tokens, tokens), 1)
    earlier = jnp.where(cols < rows, 1.0, 0.0).astype(BF)
    before = jnp.dot(earlier, total, preferred_element_type=F32)
    slots = lax.broadcasted_iota(jnp.int32, (tokens, n_local * capacity), 1)
    block = routes if turn is None else jnp.bitwise_xor(routes, turn)
    masks = []
    for k in range(top):
        slot = jnp.sum(jnp.where(named[k], before, 0.0), axis=1, keepdims=True)
        masks.append(slots == block[:, k : k + 1] * capacity + slot.astype(jnp.int32))
    return masks


def dispatch_kernel(n_local, capacity, routes_ref, gates_ref, rows_ref, out_ref):
    masks = picks_of(routes_ref[...].T, n_local, capacity)
    gates = gates_ref[...].astype(F32).T
    scaled = sum(jnp.where(m, gates[:, k : k + 1], 0.0) for k, m in enumerate(masks)).astype(BF)
    out = lax.dot_general(
        scaled, rows_ref[...], (((0,), (1,)), ((), ())), preferred_element_type=F32
    ).astype(BF)
    for e in range(n_local):
        out_ref[e] = out[e * capacity : (e + 1) * capacity]


def raw_kernel(rows_ref, down_ref, out_ref):
    out_ref[0] = jnp.dot(rows_ref[...], down_ref[...], preferred_element_type=F32).astype(BF)


def factors(g, u):
    sig = 1.0 / (1.0 + jnp.exp(-g))
    return u * sig * (1.0 + g * (1.0 - sig)), g * sig


def share_kernel(place_ref, parts_ref, gate_ref, up_ref, raw_ref, delta_ref):
    quarter = raw_ref.shape[1]
    raw = parts_ref[0].astype(F32)
    for i in range(1, parts_ref.shape[0]):
        raw = raw + parts_ref[i].astype(F32)
    raw_ref[...] = raw.astype(BF)
    here = pl.ds(pl.multiple_of(place_ref[1] * quarter, quarter), quarter)
    for_gate, for_up = factors(gate_ref[:, here].astype(F32), up_ref[:, here].astype(F32))
    gate_delta = (raw * for_gate).astype(BF)
    up_delta = (raw * for_up).astype(BF)
    delta_ref[:, :quarter] = gate_delta
    delta_ref[:, quarter:] = up_delta


def grads_kernel(own, x_ref, delta_ref, out_ref):
    n_z, n_y = out_ref.shape[:2]
    res = lax.dot_general(
        x_ref[0], delta_ref[...], (((0,), (0,)), ((), ())), preferred_element_type=F32
    )
    for i in range(n_y * n_z):
        piece = res[i * own : (i + 1) * own]
        tall = jnp.concatenate(
            [piece[:, c * 128 : (c + 1) * 128] for c in range(piece.shape[1] // 128)], axis=0
        )
        out_ref[i % n_z, i // n_z, 0] = tall.astype(BF)


def input_kernel(capacity, place_ref, raw_ref, gate_ref, up_ref, wg_ref, wu_ref, out_ref, total, side):
    step = pl.program_id(0)
    raw = raw_ref[0].astype(F32)
    u = up_ref[...].astype(F32)
    for_gate, for_up = factors(gate_ref[...].astype(F32), u)
    up_delta = raw * for_up
    dims = (((1,), (1,)), ((), ()))
    term = lax.dot_general(
        (raw * for_gate).astype(BF), wg_ref[...], dims, preferred_element_type=F32
    ) + lax.dot_general(up_delta.astype(BF), wu_ref[...], dims, preferred_element_type=F32)
    dgate = jnp.broadcast_to(jnp.sum(up_delta * u, axis=1, keepdims=True), side.shape)

    @pl.when(step == 0)
    def _():
        total[...] = term
        side[...] = dgate

    @pl.when(step > 0)
    def _():
        total[...] += term
        side[...] += dgate

    @pl.when(step == pl.num_programs(0) - 1)
    def _():
        feat = total.shape[1]
        rest = out_ref.shape[2] - feat
        for k in range(out_ref.shape[0]):
            to = jnp.bitwise_xor(place_ref[2], k)
            rows = pl.ds(pl.multiple_of(to * capacity, 8), capacity)
            out_ref[k, :, :feat] = total[rows, :].astype(BF)
            out_ref[k, :, feat:] = side[rows, :rest].astype(BF)


def combine_kernel(n_local, capacity, place_ref, routes_ref, gates_ref, *rest):
    back_refs, (rows_ref, grads_ref) = rest[:-2], rest[-2:]
    masks = [
        jnp.where(m, 1.0, 0.0).astype(BF)
        for m in picks_of(routes_ref[...].T, n_local, capacity, place_ref[2])
    ]
    feat = rows_ref.shape[0]
    back = jnp.concatenate([r[...] for r in back_refs], axis=0)
    rows_ref[...] = lax.dot_general(
        back[:, :feat], sum(masks[1:], masks[0]), (((0,), (1,)), ((), ())), preferred_element_type=F32
    ).astype(BF)
    tail = back[:, back.shape[1] - 128 :]
    gates = gates_ref[...].astype(F32)
    for k, m in enumerate(masks):
        sums = lax.dot_general(
            tail, m, (((0,), (1,)), ((), ())), preferred_element_type=F32
        )[127:128]
        grads_ref[k : k + 1, :] = (sums / gates[k : k + 1, :]).astype(BF)


def final_kernel(n_copies, own, parts_ref, gate_ref, up_ref):
    copies, n_node = parts_ref.shape[0], parts_ref.shape[1]
    for x in range(n_node):
        total = parts_ref[0, x].astype(F32)
        for i in range(1, copies):
            total = total + parts_ref[i, x].astype(F32)
        total = total * (1.0 / n_copies)
        per = total.shape[0] // own // 2
        for c in range(2 * per):
            out = gate_ref if c < per else up_ref
            out[:, x * per + c % per, :] = total[c * own : (c + 1) * own]


def params(mib=32, **more):
    return pltpu.CompilerParams(vmem_limit_bytes=mib * MIB, **more)


SMEM = pl.BlockSpec(memory_space=pltpu.SMEM)
VMEM = pl.BlockSpec(memory_space=pltpu.VMEM)


def local(token_grads, routes, gates, expert_inputs, gate_pre, up_pre, w_gate, w_up, w_down):
    tokens, top = routes.shape
    n_local = lax.axis_size("local")
    n_node = lax.axis_size("node")
    n_z, n_y = lax.axis_size("z"), lax.axis_size("y")
    n_copies = n_y * n_z
    capacity = expert_inputs.shape[3]
    feat = token_grads.shape[1]
    hidden = gate_pre.shape[4]
    quarter = hidden // n_node
    slots = n_local * capacity
    own = feat // n_copies
    wide = -(-(feat + 1) // 128) * 128
    place = jnp.stack([lax.axis_index(a) for a in ("z", "node", "local")]).astype(jnp.int32)
    gate_rows = gate_pre.reshape(slots, hidden)
    up_rows = up_pre.reshape(slots, hidden)
    x_rows = expert_inputs.reshape(slots, feat)

    outgoing = pl.pallas_call(
        functools.partial(dispatch_kernel, n_local, capacity),
        out_shape=jax.ShapeDtypeStruct((n_local, capacity, feat), BF),
        compiler_params=params(),
        name="dispatch",
    )(routes.T, gates.T, token_grads.T)
    arrived = lax.all_to_all(outgoing, "local", split_axis=0, concat_axis=0, tiled=True)

    node_x = lax.all_gather(x_rows, "node", axis=0, tiled=False)

    raw_parts = pl.pallas_call(
        raw_kernel,
        grid=(n_node,),
        in_specs=[
            pl.BlockSpec((slots, feat), lambda i: (0, 0)),
            pl.BlockSpec((feat, quarter), lambda i: (0, i)),
        ],
        out_specs=pl.BlockSpec((1, slots, quarter), lambda i: (i, 0, 0)),
        out_shape=jax.ShapeDtypeStruct((n_node, slots, quarter), BF),
        compiler_params=params(),
        name="raw",
    )(arrived.reshape(slots, feat), w_down[0].T)
    raw_shares = lax.all_to_all(raw_parts, "node", split_axis=0, concat_axis=0, tiled=True)

    raw_share, deltas = pl.pallas_call(
        share_kernel,
        in_specs=[SMEM, VMEM, VMEM, VMEM],
        out_shape=[
            jax.ShapeDtypeStruct((slots, quarter), BF),
            jax.ShapeDtypeStruct((slots, 2 * quarter), BF),
        ],
        compiler_params=params(),
        name="share",
    )(place, raw_shares, gate_rows, up_rows)

    tall = own * 2 * quarter // 128
    grads = pl.pallas_call(
        functools.partial(grads_kernel, own),
        grid=(n_node,),
        in_specs=[
            pl.BlockSpec((1, slots, feat), lambda i: (i, 0, 0)),
            pl.BlockSpec((slots, 2 * quarter), lambda i: (0, 0)),
        ],
        out_specs=pl.BlockSpec((n_z, n_y, 1, tall, 128), lambda i: (0, 0, i, 0, 0)),
        out_shape=jax.ShapeDtypeStruct((n_z, n_y, n_node, tall, 128), BF),
        compiler_params=params(),
        name="grads",
    )(node_x, deltas)
    z_sum = lax.psum_scatter(
        grads.reshape(n_z * n_y * n_node * tall, 128), "z", scatter_dimension=0, tiled=True
    )

    raw_share, _ = lax.optimization_barrier((raw_share, grads))
    raw = lax.all_gather(raw_share, "node", axis=0, tiled=False)
    slot_input = pl.pallas_call(
        functools.partial(input_kernel, capacity),
        grid=(n_node,),
        in_specs=[
            SMEM,
            pl.BlockSpec((1, slots, quarter), lambda i: (i, 0, 0)),
            pl.BlockSpec((slots, quarter), lambda i: (0, i)),
            pl.BlockSpec((slots, quarter), lambda i: (0, i)),
            pl.BlockSpec((feat, quarter), lambda i: (0, i)),
            pl.BlockSpec((feat, quarter), lambda i: (0, i)),
        ],
        out_specs=pl.BlockSpec((n_local, capacity, wide), lambda i: (0, 0, 0)),
        out_shape=jax.ShapeDtypeStruct((n_local, capacity, wide), BF),
        scratch_shapes=[pltpu.VMEM((slots, feat), F32), pltpu.VMEM((slots, 128), F32)],
        compiler_params=params(),
        name="slot_input",
    )(place, raw, gate_rows, up_rows, w_gate[0], w_up[0])
    back = [slot_input[0]] + [
        lax.ppermute(slot_input[k], "local", [(i, i ^ k) for i in range(n_local)])
        for k in range(1, n_local)
    ]
    input_grads, gate_grads = pl.pallas_call(
        functools.partial(combine_kernel, n_local, capacity),
        in_specs=[SMEM] + [VMEM] * (2 + n_local),
        out_shape=[
            jax.ShapeDtypeStruct((feat, tokens), BF),
            jax.ShapeDtypeStruct((top, tokens), BF),
        ],
        compiler_params=params(),
        name="combine",
    )(place, routes.T, gates.T, *back)

    z_sum, input_grads, gate_grads = lax.optimization_barrier((z_sum, input_grads, gate_grads))
    parts = lax.all_to_all(
        z_sum.reshape(n_y * n_node, tall, 128),
        ("y", "node"),
        split_axis=0,
        concat_axis=0,
        tiled=True,
    )
    gate_sum, up_sum = pl.pallas_call(
        functools.partial(final_kernel, n_copies, own),
        out_shape=[jax.ShapeDtypeStruct((own, hidden // 128, 128), F32)] * 2,
        compiler_params=params(),
        name="final",
    )(parts.reshape(n_y, n_node, tall, 128))
    rows = own * hidden // 128
    return (
        input_grads.T,
        gate_grads.T,
        gate_sum.reshape(1, 1, rows, 128),
        up_sum.reshape(1, 1, rows, 128),
    )


def solution(mesh):
    shape = mesh.devices.shape
    cut = Mesh(mesh.devices.reshape(*CUT, shape[1], shape[2]), ("y", "z", "node", "local"))
    replica = ("y", "z")
    placed = (
        P((*replica, "local"), "node"),
        P((*replica, "local"), None),
        P((*replica, "local"), None),
        P(replica, "local", None, None, "node"),
        P(replica, "local", None, None, None),
        P(replica, "local", None, None, None),
        P("local", "node", None),
        P("local", "node", None),
        P("local", None, "node"),
    )
    return jax.shard_map(
        local,
        mesh=cut,
        in_specs=placed,
        out_specs=(
            P((*replica, "local"), "node"),
            P((*replica, "local"), None),
            P("local", "node", replica, None),
            P("local", "node", replica, None),
        ),
        check_vma=False,
    )
```

```python
import functools

import jax
import jax.numpy as jnp
from jax import lax
from jax.experimental import pallas as pl
from jax.experimental.pallas import tpu as pltpu
from jax.sharding import Mesh
from jax.sharding import PartitionSpec as P

BF = jnp.bfloat16
F32 = jnp.float32
MIB = 1 << 20


CUT = (4, 12)


def picks_of(routes, n_local, capacity, turn=None):
    tokens, top = routes.shape
    lanes = lax.broadcasted_iota(jnp.int32, (tokens, 128), 1)
    named = [(lanes == routes[:, k : k + 1]) for k in range(top)]
    total = sum(jnp.where(n, 1.0, 0.0) for n in named).astype(BF)
    rows = lax.broadcasted_iota(jnp.int32, (tokens, tokens), 0)
    cols = lax.broadcasted_iota(jnp.int32, (tokens, tokens), 1)
    earlier = jnp.where(cols < rows, 1.0, 0.0).astype(BF)
    before = jnp.dot(earlier, total, preferred_element_type=F32)
    slots = lax.broadcasted_iota(jnp.int32, (tokens, n_local * capacity), 1)
    block = routes if turn is None else jnp.bitwise_xor(routes, turn)
    masks = []
    for k in range(top):
        slot = jnp.sum(jnp.where(named[k], before, 0.0), axis=1, keepdims=True)
        masks.append(slots == block[:, k : k + 1] * capacity + slot.astype(jnp.int32))
    return masks


def dispatch_kernel(n_local, capacity, routes_ref, gates_ref, rows_ref, out_ref):
    masks = picks_of(routes_ref[...].T, n_local, capacity)
    gates = gates_ref[...].astype(F32).T
    scaled = sum(jnp.where(m, gates[:, k : k + 1], 0.0) for k, m in enumerate(masks)).astype(BF)
    out = lax.dot_general(
        scaled, rows_ref[...], (((0,), (1,)), ((), ())), preferred_element_type=F32
    ).astype(BF)
    for e in range(n_local):
        out_ref[e] = out[e * capacity : (e + 1) * capacity]


def raw_kernel(rows_ref, down_ref, out_ref):
    out_ref[0] = jnp.dot(rows_ref[...], down_ref[...], preferred_element_type=F32).astype(BF)


def factors(g, u):
    sig = 1.0 / (1.0 + jnp.exp(-g))
    return u * sig * (1.0 + g * (1.0 - sig)), g * sig


def share_kernel(place_ref, parts_ref, gate_ref, up_ref, raw_ref, delta_ref):
    quarter = raw_ref.shape[1]
    raw = parts_ref[0].astype(F32)
    for i in range(1, parts_ref.shape[0]):
        raw = raw + parts_ref[i].astype(F32)
    raw_ref[...] = raw.astype(BF)
    here = pl.ds(pl.multiple_of(place_ref[1] * quarter, quarter), quarter)
    for_gate, for_up = factors(gate_ref[:, here].astype(F32), up_ref[:, here].astype(F32))
    gate_delta = (raw * for_gate).astype(BF)
    up_delta = (raw * for_up).astype(BF)
    delta_ref[:, :quarter] = gate_delta
    delta_ref[:, quarter:] = up_delta


def grads_kernel(own, place_ref, own_ref, prev_ref, next_ref, half_refs, delta_ref, out_ref):
    step = pl.program_id(0)
    n_z, n_y = out_ref.shape[:2]

    def block(x):
        res = lax.dot_general(
            x, delta_ref[...], (((0,), (0,)), ((), ())), preferred_element_type=F32
        )
        for i in range(n_y * n_z):
            piece = res[i * own : (i + 1) * own]
            tall = jnp.concatenate(
                [piece[:, c * 128 : (c + 1) * 128] for c in range(piece.shape[1] // 128)], axis=0
            )
            out_ref[i % n_z, i // n_z, 0] = tall.astype(BF)

    for k, ref in enumerate((own_ref, prev_ref, next_ref)):

        @pl.when(step == k)
        def _(ref=ref):
            block(ref[...])

    @pl.when(step == 3)
    def _():
        block(jnp.concatenate([half_refs[0][...], half_refs[1][...]], axis=0))


def input_kernel(capacity, place_ref, raw_ref, gate_ref, up_ref, wg_ref, wu_ref, out_ref, total, side):
    step = pl.program_id(0)
    raw = raw_ref[0].astype(F32)
    u = up_ref[...].astype(F32)
    for_gate, for_up = factors(gate_ref[...].astype(F32), u)
    up_delta = raw * for_up
    dims = (((1,), (1,)), ((), ()))
    term = lax.dot_general(
        (raw * for_gate).astype(BF), wg_ref[...], dims, preferred_element_type=F32
    ) + lax.dot_general(up_delta.astype(BF), wu_ref[...], dims, preferred_element_type=F32)
    dgate = jnp.broadcast_to(jnp.sum(up_delta * u, axis=1, keepdims=True), side.shape)

    @pl.when(step == 0)
    def _():
        total[...] = term
        side[...] = dgate

    @pl.when(step > 0)
    def _():
        total[...] += term
        side[...] += dgate

    @pl.when(step == pl.num_programs(0) - 1)
    def _():
        feat = total.shape[1]
        rest = out_ref.shape[2] - feat
        for k in range(out_ref.shape[0]):
            to = jnp.bitwise_xor(place_ref[2], k)
            rows = pl.ds(pl.multiple_of(to * capacity, 8), capacity)
            out_ref[k, :, :feat] = total[rows, :].astype(BF)
            out_ref[k, :, feat:] = side[rows, :rest].astype(BF)


def combine_kernel(n_local, capacity, place_ref, routes_ref, gates_ref, *rest):
    back_refs, (rows_ref, grads_ref) = rest[:-2], rest[-2:]
    masks = [
        jnp.where(m, 1.0, 0.0).astype(BF)
        for m in picks_of(routes_ref[...].T, n_local, capacity, place_ref[2])
    ]
    feat = rows_ref.shape[0]
    back = jnp.concatenate([r[...] for r in back_refs], axis=0)
    rows_ref[...] = lax.dot_general(
        back[:, :feat], sum(masks[1:], masks[0]), (((0,), (1,)), ((), ())), preferred_element_type=F32
    ).astype(BF)
    tail = back[:, back.shape[1] - 128 :]
    gates = gates_ref[...].astype(F32)
    for k, m in enumerate(masks):
        sums = lax.dot_general(
            tail, m, (((0,), (1,)), ((), ())), preferred_element_type=F32
        )[127:128]
        grads_ref[k : k + 1, :] = (sums / gates[k : k + 1, :]).astype(BF)


def final_kernel(n_copies, own, parts_ref, gate_ref, up_ref):
    copies, n_node = parts_ref.shape[0], parts_ref.shape[1]
    for x in range(n_node):
        total = parts_ref[0, x].astype(F32)
        for i in range(1, copies):
            total = total + parts_ref[i, x].astype(F32)
        total = total * (1.0 / n_copies)
        per = total.shape[0] // own // 2
        for c in range(2 * per):
            out = gate_ref if c < per else up_ref
            out[:, x * per + c % per, :] = total[c * own : (c + 1) * own]


def params(mib=32, **more):
    return pltpu.CompilerParams(vmem_limit_bytes=mib * MIB, **more)


def ring(x, axis, step):
    n = lax.axis_size(axis)
    return lax.ppermute(x, axis, [(i, (i + step) % n) for i in range(n)])


SMEM = pl.BlockSpec(memory_space=pltpu.SMEM)
VMEM = pl.BlockSpec(memory_space=pltpu.VMEM)


def local(token_grads, routes, gates, expert_inputs, gate_pre, up_pre, w_gate, w_up, w_down):
    tokens, top = routes.shape
    n_local = lax.axis_size("local")
    n_node = lax.axis_size("node")
    n_z, n_y = lax.axis_size("z"), lax.axis_size("y")
    n_copies = n_y * n_z
    capacity = expert_inputs.shape[3]
    feat = token_grads.shape[1]
    hidden = gate_pre.shape[4]
    quarter = hidden // n_node
    slots = n_local * capacity
    own = feat // n_copies
    wide = -(-(feat + 1) // 128) * 128
    place = jnp.stack([lax.axis_index(a) for a in ("z", "node", "local")]).astype(jnp.int32)
    gate_rows = gate_pre.reshape(slots, hidden)
    up_rows = up_pre.reshape(slots, hidden)
    x_rows = expert_inputs.reshape(slots, feat)

    outgoing = pl.pallas_call(
        functools.partial(dispatch_kernel, n_local, capacity),
        out_shape=jax.ShapeDtypeStruct((n_local, capacity, feat), BF),
        compiler_params=params(),
        name="dispatch",
    )(routes.T, gates.T, token_grads.T)
    arrived = lax.all_to_all(outgoing, "local", split_axis=0, concat_axis=0, tiled=True)

    x_rows, _ = lax.optimization_barrier((x_rows, outgoing))
    x_prev, x_next = ring(x_rows, "node", 1), ring(x_rows, "node", -1)

    raw_parts = pl.pallas_call(
        raw_kernel,
        grid=(n_node,),
        in_specs=[
            pl.BlockSpec((slots, feat), lambda i: (0, 0)),
            pl.BlockSpec((feat, quarter), lambda i: (0, i)),
        ],
        out_specs=pl.BlockSpec((1, slots, quarter), lambda i: (i, 0, 0)),
        out_shape=jax.ShapeDtypeStruct((n_node, slots, quarter), BF),
        compiler_params=params(),
        name="raw",
    )(arrived.reshape(slots, feat), w_down[0].T)
    raw_shares = lax.all_to_all(raw_parts, "node", split_axis=0, concat_axis=0, tiled=True)

    half = slots // 2
    x_prev, x_next, _ = lax.optimization_barrier((x_prev, x_next, raw_parts))
    x_across = (ring(x_prev[:half], "node", 1), ring(x_next[half:], "node", -1))

    raw_share, deltas = pl.pallas_call(
        share_kernel,
        in_specs=[SMEM, VMEM, VMEM, VMEM],
        out_shape=[
            jax.ShapeDtypeStruct((slots, quarter), BF),
            jax.ShapeDtypeStruct((slots, 2 * quarter), BF),
        ],
        compiler_params=params(),
        name="share",
    )(place, raw_shares, gate_rows, up_rows)

    tall = own * 2 * quarter // 128
    grads = pl.pallas_call(
        functools.partial(grads_kernel, own),
        grid_spec=pltpu.PrefetchScalarGridSpec(
            num_scalar_prefetch=1,
            grid=(n_node,),
            in_specs=[
                pl.BlockSpec((slots, feat), lambda i, p: (0, 0)),
                pl.BlockSpec((slots, feat), lambda i, p: (0, 0)),
                pl.BlockSpec((slots, feat), lambda i, p: (0, 0)),
                [pl.BlockSpec((half, feat), lambda i, p: (0, 0))] * 2,
                pl.BlockSpec((slots, 2 * quarter), lambda i, p: (0, 0)),
            ],
            out_specs=pl.BlockSpec(
                (n_z, n_y, 1, tall, 128),
                lambda i, p: (0, 0, (p[1] + jnp.where(i < 2, 3 * i, i - 1)) % n_node, 0, 0),
            ),
        ),
        out_shape=jax.ShapeDtypeStruct((n_z, n_y, n_node, tall, 128), BF),
        compiler_params=params(),
        name="grads",
    )(place, x_rows, x_prev, x_next, list(x_across), deltas)
    z_sum = lax.psum_scatter(
        grads.reshape(n_z * n_y * n_node * tall, 128), "z", scatter_dimension=0, tiled=True
    )

    raw_share, _ = lax.optimization_barrier((raw_share, grads))
    raw = lax.all_gather(raw_share, "node", axis=0, tiled=False)
    slot_input = pl.pallas_call(
        functools.partial(input_kernel, capacity),
        grid=(n_node,),
        in_specs=[
            SMEM,
            pl.BlockSpec((1, slots, quarter), lambda i: (i, 0, 0)),
            pl.BlockSpec((slots, quarter), lambda i: (0, i)),
            pl.BlockSpec((slots, quarter), lambda i: (0, i)),
            pl.BlockSpec((feat, quarter), lambda i: (0, i)),
            pl.BlockSpec((feat, quarter), lambda i: (0, i)),
        ],
        out_specs=pl.BlockSpec((n_local, capacity, wide), lambda i: (0, 0, 0)),
        out_shape=jax.ShapeDtypeStruct((n_local, capacity, wide), BF),
        scratch_shapes=[pltpu.VMEM((slots, feat), F32), pltpu.VMEM((slots, 128), F32)],
        compiler_params=params(),
        name="slot_input",
    )(place, raw, gate_rows, up_rows, w_gate[0], w_up[0])
    back = [slot_input[0]] + [
        lax.ppermute(slot_input[k], "local", [(i, i ^ k) for i in range(n_local)])
        for k in range(1, n_local)
    ]
    input_grads, gate_grads = pl.pallas_call(
        functools.partial(combine_kernel, n_local, capacity),
        in_specs=[SMEM] + [VMEM] * (2 + n_local),
        out_shape=[
            jax.ShapeDtypeStruct((feat, tokens), BF),
            jax.ShapeDtypeStruct((top, tokens), BF),
        ],
        compiler_params=params(),
        name="combine",
    )(place, routes.T, gates.T, *back)

    z_sum, input_grads, gate_grads = lax.optimization_barrier((z_sum, input_grads, gate_grads))
    parts = lax.all_to_all(
        z_sum.reshape(n_y * n_node, tall, 128),
        ("y", "node"),
        split_axis=0,
        concat_axis=0,
        tiled=True,
    )
    gate_sum, up_sum = pl.pallas_call(
        functools.partial(final_kernel, n_copies, own),
        out_shape=[jax.ShapeDtypeStruct((own, hidden // 128, 128), F32)] * 2,
        compiler_params=params(),
        name="final",
    )(parts.reshape(n_y, n_node, tall, 128))
    rows = own * hidden // 128
    return (
        input_grads.T,
        gate_grads.T,
        gate_sum.reshape(1, 1, rows, 128),
        up_sum.reshape(1, 1, rows, 128),
    )


def solution(mesh):
    shape = mesh.devices.shape
    cut = Mesh(mesh.devices.reshape(*CUT, shape[1], shape[2]), ("y", "z", "node", "local"))
    replica = ("y", "z")
    placed = (
        P((*replica, "local"), "node"),
        P((*replica, "local"), None),
        P((*replica, "local"), None),
        P(replica, "local", None, None, "node"),
        P(replica, "local", None, None, None),
        P(replica, "local", None, None, None),
        P("local", "node", None),
        P("local", "node", None),
        P("local", None, "node"),
    )
    return jax.shard_map(
        local,
        mesh=cut,
        in_specs=placed,
        out_specs=(
            P((*replica, "local"), "node"),
            P((*replica, "local"), None),
            P("local", "node", replica, None),
            P("local", "node", replica, None),
        ),
        check_vma=False,
    )
```

```python
import functools

import jax
import jax.numpy as jnp
from jax import lax
from jax.experimental import pallas as pl
from jax.experimental.pallas import tpu as pltpu
from jax.sharding import Mesh
from jax.sharding import PartitionSpec as P

BF = jnp.bfloat16
F32 = jnp.float32
MIB = 1 << 20


CUT = (4, 3, 4)


def picks_of(routes, n_local, capacity, turn=None):
    tokens, top = routes.shape
    lanes = lax.broadcasted_iota(jnp.int32, (tokens, 128), 1)
    named = [(lanes == routes[:, k : k + 1]) for k in range(top)]
    total = sum(jnp.where(n, 1.0, 0.0) for n in named).astype(BF)
    rows = lax.broadcasted_iota(jnp.int32, (tokens, tokens), 0)
    cols = lax.broadcasted_iota(jnp.int32, (tokens, tokens), 1)
    earlier = jnp.where(cols < rows, 1.0, 0.0).astype(BF)
    before = jnp.dot(earlier, total, preferred_element_type=F32)
    slots = lax.broadcasted_iota(jnp.int32, (tokens, n_local * capacity), 1)
    block = routes if turn is None else jnp.bitwise_xor(routes, turn)
    masks = []
    for k in range(top):
        slot = jnp.sum(jnp.where(named[k], before, 0.0), axis=1, keepdims=True)
        masks.append(slots == block[:, k : k + 1] * capacity + slot.astype(jnp.int32))
    return masks


def dispatch_kernel(n_local, capacity, routes_ref, gates_ref, rows_ref, out_ref):
    masks = picks_of(routes_ref[...].T, n_local, capacity)
    gates = gates_ref[...].astype(F32).T
    scaled = sum(jnp.where(m, gates[:, k : k + 1], 0.0) for k, m in enumerate(masks)).astype(BF)
    out = lax.dot_general(
        scaled, rows_ref[...], (((0,), (1,)), ((), ())), preferred_element_type=F32
    ).astype(BF)
    for e in range(n_local):
        out_ref[e] = out[e * capacity : (e + 1) * capacity]


def raw_kernel(rows_ref, down_ref, out_ref):
    out_ref[0] = jnp.dot(rows_ref[...], down_ref[...], preferred_element_type=F32).astype(BF)


def factors(g, u):
    sig = 1.0 / (1.0 + jnp.exp(-g))
    return u * sig * (1.0 + g * (1.0 - sig)), g * sig


def early_kernel(n_y, place_ref, x_ref, out_ref):
    y = place_ref[0]
    feat = x_ref.shape[1]
    part = feat // n_y
    at = lax.broadcasted_iota(jnp.int32, (feat, part), 0) - lax.broadcasted_iota(
        jnp.int32, (feat, part), 1
    )
    x = x_ref[...]
    for k in range(n_y):
        first = jnp.bitwise_and(y + k, n_y - 1) * part
        chosen = jnp.where(at == first, 1.0, 0.0).astype(BF)
        out_ref[k] = jnp.dot(x, chosen, preferred_element_type=F32).astype(BF)


def share_kernel(place_ref, parts_ref, gate_ref, up_ref, raw_ref, delta_ref):
    quarter = raw_ref.shape[1]
    raw = parts_ref[0].astype(F32)
    for i in range(1, parts_ref.shape[0]):
        raw = raw + parts_ref[i].astype(F32)
    raw_ref[...] = raw.astype(BF)
    here = pl.ds(pl.multiple_of(place_ref[1] * quarter, quarter), quarter)
    for_gate, for_up = factors(gate_ref[:, here].astype(F32), up_ref[:, here].astype(F32))
    gate_delta = (raw * for_gate).astype(BF)
    up_delta = (raw * for_up).astype(BF)
    for k in range(delta_ref.shape[0]):
        delta_ref[k, :, :quarter] = gate_delta
        delta_ref[k, :, quarter:] = up_delta


def grads_kernel(own, place_ref, delta_ref, x_ref, out_ref, ordered):
    n_y, slots, _ = delta_ref.shape
    for k in range(n_y):
        copy = jnp.bitwise_and(place_ref[0] + n_y - k, n_y - 1)
        ordered[k * slots : (k + 1) * slots] = delta_ref[copy]
    d = ordered[...]
    n_zl, n_node, n_zh = out_ref.shape[:3]
    for b in range(n_node):
        res = lax.dot_general(
            x_ref[b], d, (((0,), (0,)), ((), ())), preferred_element_type=F32
        )
        for i in range(n_zh * n_zl):
            piece = res[i * own : (i + 1) * own]
            tall = jnp.concatenate(
                [piece[:, c * 128 : (c + 1) * 128] for c in range(piece.shape[1] // 128)], axis=0
            )
            out_ref[i % n_zl, b, i // n_zl] = tall.astype(BF)


def near_kernel(place_ref, parts_ref, out_ref):
    n_zl, n_node, n_zh = parts_ref.shape[:3]
    for k in range(n_zh):
        to = place_ref[3] + k
        to = jnp.where(to >= n_zh, to - n_zh, to)
        for x in range(n_node):
            total = parts_ref[0, x, to].astype(F32)
            for i in range(1, n_zl):
                total = total + parts_ref[i, x, to].astype(F32)
            out_ref[k, x] = total.astype(BF)


def input_kernel(capacity, place_ref, raw_ref, gate_ref, up_ref, wg_ref, wu_ref, out_ref, total, side):
    step = pl.program_id(0)
    raw = raw_ref[0].astype(F32)
    u = up_ref[...].astype(F32)
    for_gate, for_up = factors(gate_ref[...].astype(F32), u)
    up_delta = raw * for_up
    dims = (((1,), (1,)), ((), ()))
    term = lax.dot_general(
        (raw * for_gate).astype(BF), wg_ref[...], dims, preferred_element_type=F32
    ) + lax.dot_general(up_delta.astype(BF), wu_ref[...], dims, preferred_element_type=F32)
    dgate = jnp.broadcast_to(jnp.sum(up_delta * u, axis=1, keepdims=True), side.shape)

    @pl.when(step == 0)
    def _():
        total[...] = term
        side[...] = dgate

    @pl.when(step > 0)
    def _():
        total[...] += term
        side[...] += dgate

    @pl.when(step == pl.num_programs(0) - 1)
    def _():
        feat = total.shape[1]
        rest = out_ref.shape[2] - feat
        for k in range(out_ref.shape[0]):
            to = jnp.bitwise_xor(place_ref[2], k)
            rows = pl.ds(pl.multiple_of(to * capacity, 8), capacity)
            out_ref[k, :, :feat] = total[rows, :].astype(BF)
            out_ref[k, :, feat:] = side[rows, :rest].astype(BF)


def combine_kernel(n_local, capacity, place_ref, routes_ref, gates_ref, *rest):
    back_refs, (rows_ref, grads_ref) = rest[:-2], rest[-2:]
    masks = [
        jnp.where(m, 1.0, 0.0).astype(BF)
        for m in picks_of(routes_ref[...].T, n_local, capacity, place_ref[2])
    ]
    feat = rows_ref.shape[0]
    back = jnp.concatenate([r[...] for r in back_refs], axis=0)
    rows_ref[...] = lax.dot_general(
        back[:, :feat], sum(masks[1:], masks[0]), (((0,), (1,)), ((), ())), preferred_element_type=F32
    ).astype(BF)
    tail = back[:, back.shape[1] - 128 :]
    gates = gates_ref[...].astype(F32)
    for k, m in enumerate(masks):
        sums = lax.dot_general(
            tail, m, (((0,), (1,)), ((), ())), preferred_element_type=F32
        )[127:128]
        grads_ref[k : k + 1, :] = (sums / gates[k : k + 1, :]).astype(BF)


def final_kernel(n_copies, own, *refs):
    parts_refs, (gate_ref, up_ref) = refs[:-2], refs[-2:]
    for x in range(parts_refs[0].shape[0]):
        total = parts_refs[0][x].astype(F32)
        for ref in parts_refs[1:]:
            total = total + ref[x].astype(F32)
        total = total * (1.0 / n_copies)
        per = total.shape[0] // own // 2
        for c in range(2 * per):
            out = gate_ref if c < per else up_ref
            out[:, x * per + c % per, :] = total[c * own : (c + 1) * own]


def params(mib=32, **more):
    return pltpu.CompilerParams(vmem_limit_bytes=mib * MIB, **more)


def ring(x, axis, step):
    n = lax.axis_size(axis)
    return lax.ppermute(x, axis, [(i, (i + step) % n) for i in range(n)])


SMEM = pl.BlockSpec(memory_space=pltpu.SMEM)
VMEM = pl.BlockSpec(memory_space=pltpu.VMEM)


def local(token_grads, routes, gates, expert_inputs, gate_pre, up_pre, w_gate, w_up, w_down):
    tokens, top = routes.shape
    n_local = lax.axis_size("local")
    n_node = lax.axis_size("node")
    n_zl, n_zh, n_y = lax.axis_size("zl"), lax.axis_size("zh"), lax.axis_size("y")
    n_copies = n_y * n_zh * n_zl
    capacity = expert_inputs.shape[3]
    feat = token_grads.shape[1]
    hidden = gate_pre.shape[4]
    quarter = hidden // n_node
    slots = n_local * capacity
    own = feat // n_copies
    part = feat // n_y
    wide = -(-(feat + 1) // 128) * 128
    place = jnp.stack([lax.axis_index(a) for a in ("y", "node", "local", "zh")]).astype(jnp.int32)
    gate_rows = gate_pre.reshape(slots, hidden)
    up_rows = up_pre.reshape(slots, hidden)
    x_rows = expert_inputs.reshape(slots, feat)

    outgoing = pl.pallas_call(
        functools.partial(dispatch_kernel, n_local, capacity),
        out_shape=jax.ShapeDtypeStruct((n_local, capacity, feat), BF),
        compiler_params=params(),
        name="dispatch",
    )(routes.T, gates.T, token_grads.T)
    arrived = lax.all_to_all(outgoing, "local", split_axis=0, concat_axis=0, tiled=True)

    x_rows, _ = lax.optimization_barrier((x_rows, outgoing))
    slabs = pl.pallas_call(
        functools.partial(early_kernel, n_y),
        in_specs=[SMEM, VMEM],
        out_shape=jax.ShapeDtypeStruct((n_y, slots, part), BF),
        compiler_params=params(),
        name="early",
    )(place, x_rows)
    copies_x = [slabs[0]] + [ring(slabs[k], "y", k) for k in range(1, n_y)]

    arrived, copies_x[1], copies_x[3] = lax.optimization_barrier(
        (arrived, copies_x[1], copies_x[3])
    )
    raw_parts = pl.pallas_call(
        raw_kernel,
        grid=(n_node,),
        in_specs=[
            pl.BlockSpec((slots, feat), lambda i: (0, 0)),
            pl.BlockSpec((feat, quarter), lambda i: (0, i)),
        ],
        out_specs=pl.BlockSpec((1, slots, quarter), lambda i: (i, 0, 0)),
        out_shape=jax.ShapeDtypeStruct((n_node, slots, quarter), BF),
        compiler_params=params(),
        name="raw",
    )(arrived.reshape(slots, feat), w_down[0].T)
    raw_shares = lax.all_to_all(raw_parts, "node", split_axis=0, concat_axis=0, tiled=True)

    copies_x[2], raw_shares = lax.optimization_barrier((copies_x[2], raw_shares))
    node_x = lax.all_gather(jnp.concatenate(copies_x, axis=0), "node", axis=0, tiled=False)

    raw_share, deltas = pl.pallas_call(
        share_kernel,
        in_specs=[SMEM, VMEM, VMEM, VMEM],
        out_shape=[
            jax.ShapeDtypeStruct((slots, quarter), BF),
            jax.ShapeDtypeStruct((n_y, slots, 2 * quarter), BF),
        ],
        compiler_params=params(),
        name="share",
    )(place, raw_shares, gate_rows, up_rows)
    all_deltas = lax.all_to_all(deltas, "y", split_axis=0, concat_axis=0, tiled=True)

    raw = lax.all_gather(raw_share, "node", axis=0, tiled=False)
    slot_input = pl.pallas_call(
        functools.partial(input_kernel, capacity),
        grid=(n_node,),
        in_specs=[
            SMEM,
            pl.BlockSpec((1, slots, quarter), lambda i: (i, 0, 0)),
            pl.BlockSpec((slots, quarter), lambda i: (0, i)),
            pl.BlockSpec((slots, quarter), lambda i: (0, i)),
            pl.BlockSpec((feat, quarter), lambda i: (0, i)),
            pl.BlockSpec((feat, quarter), lambda i: (0, i)),
        ],
        out_specs=pl.BlockSpec((n_local, capacity, wide), lambda i: (0, 0, 0)),
        out_shape=jax.ShapeDtypeStruct((n_local, capacity, wide), BF),
        scratch_shapes=[pltpu.VMEM((slots, feat), F32), pltpu.VMEM((slots, 128), F32)],
        compiler_params=params(),
        name="slot_input",
    )(place, raw, gate_rows, up_rows, w_gate[0], w_up[0])
    all_deltas, slot_input = lax.optimization_barrier((all_deltas, slot_input))

    tall = own * 2 * quarter // 128
    grads = pl.pallas_call(
        functools.partial(grads_kernel, own),
        in_specs=[SMEM, VMEM, VMEM],
        out_shape=jax.ShapeDtypeStruct((n_zl, n_node, n_zh, tall, 128), BF),
        scratch_shapes=[pltpu.VMEM((n_y * slots, 2 * quarter), BF)],
        compiler_params=params(),
        name="grads",
    )(place, all_deltas, node_x)
    near = lax.all_to_all(
        grads.reshape(n_zl * n_node, n_zh, tall, 128),
        ("zl", "node"),
        split_axis=0,
        concat_axis=0,
        tiled=True,
    )
    back = [slot_input[0]] + [
        lax.ppermute(slot_input[k], "local", [(i, i ^ k) for i in range(n_local)])
        for k in range(1, n_local)
    ]
    input_grads, gate_grads = pl.pallas_call(
        functools.partial(combine_kernel, n_local, capacity),
        in_specs=[SMEM] + [VMEM] * (2 + n_local),
        out_shape=[
            jax.ShapeDtypeStruct((feat, tokens), BF),
            jax.ShapeDtypeStruct((top, tokens), BF),
        ],
        compiler_params=params(),
        name="combine",
    )(place, routes.T, gates.T, *back)

    near, input_grads, gate_grads = lax.optimization_barrier((near, input_grads, gate_grads))
    near_sum = pl.pallas_call(
        near_kernel,
        in_specs=[SMEM, VMEM],
        out_shape=jax.ShapeDtypeStruct((n_zh, n_node, tall, 128), BF),
        compiler_params=params(),
        name="near_sum",
    )(place, near.reshape(n_zl, n_node, n_zh, tall, 128))
    parts = [near_sum[0]] + [ring(near_sum[k], "zh", k) for k in range(1, n_zh)]
    gate_sum, up_sum = pl.pallas_call(
        functools.partial(final_kernel, n_copies, own),
        out_shape=[jax.ShapeDtypeStruct((own, hidden // 128, 128), F32)] * 2,
        compiler_params=params(),
        name="final",
    )(*parts)
    rows = own * hidden // 128
    return (
        input_grads.T,
        gate_grads.T,
        gate_sum.reshape(1, 1, rows, 128),
        up_sum.reshape(1, 1, rows, 128),
    )


def solution(mesh):
    shape = mesh.devices.shape
    cut = Mesh(mesh.devices.reshape(*CUT, shape[1], shape[2]), ("y", "zh", "zl", "node", "local"))
    replica = ("y", "zh", "zl")
    placed = (
        P((*replica, "local"), "node"),
        P((*replica, "local"), None),
        P((*replica, "local"), None),
        P(replica, "local", None, None, "node"),
        P(replica, "local", None, None, None),
        P(replica, "local", None, None, None),
        P("local", "node", None),
        P("local", "node", None),
        P("local", None, "node"),
    )
    return jax.shard_map(
        local,
        mesh=cut,
        in_specs=placed,
        out_specs=(
            P((*replica, "local"), "node"),
            P((*replica, "local"), None),
            P("local", "node", replica, None),
            P("local", "node", replica, None),
        ),
        check_vma=False,
    )
```

```python
import functools

import jax
import jax.numpy as jnp
from jax import lax
from jax.experimental import pallas as pl
from jax.experimental.pallas import tpu as pltpu
from jax.sharding import Mesh
from jax.sharding import PartitionSpec as P

BF = jnp.bfloat16
F32 = jnp.float32
MIB = 1 << 20


CUT = (4, 12)


def picks_of(routes, n_local, capacity, turn=None):
    tokens, top = routes.shape
    lanes = lax.broadcasted_iota(jnp.int32, (tokens, 128), 1)
    named = [(lanes == routes[:, k : k + 1]) for k in range(top)]
    total = sum(jnp.where(n, 1.0, 0.0) for n in named).astype(BF)
    rows = lax.broadcasted_iota(jnp.int32, (tokens, tokens), 0)
    cols = lax.broadcasted_iota(jnp.int32, (tokens, tokens), 1)
    earlier = jnp.where(cols < rows, 1.0, 0.0).astype(BF)
    before = jnp.dot(earlier, total, preferred_element_type=F32)
    slots = lax.broadcasted_iota(jnp.int32, (tokens, n_local * capacity), 1)
    block = routes if turn is None else jnp.bitwise_xor(routes, turn)
    masks = []
    for k in range(top):
        slot = jnp.sum(jnp.where(named[k], before, 0.0), axis=1, keepdims=True)
        masks.append(slots == block[:, k : k + 1] * capacity + slot.astype(jnp.int32))
    return masks


def dispatch_kernel(
    n_local, capacity, routes_in, gates_in, rows_in, out_ref, routes_ref, gates_ref, rows_ref, sems
):
    copies = [
        pltpu.make_async_copy(routes_in, routes_ref, sems.at[0]),
        pltpu.make_async_copy(gates_in, gates_ref, sems.at[1]),
        pltpu.make_async_copy(rows_in, rows_ref, sems.at[2]),
    ]
    for copy in copies:
        copy.start()
    copies[0].wait()
    masks = picks_of(routes_ref[...].T, n_local, capacity)
    copies[1].wait()
    gates = gates_ref[...].astype(F32).T
    scaled = sum(jnp.where(m, gates[:, k : k + 1], 0.0) for k, m in enumerate(masks)).astype(BF)
    copies[2].wait()
    out = lax.dot_general(
        scaled, rows_ref[...], (((0,), (1,)), ((), ())), preferred_element_type=F32
    ).astype(BF)
    for e in range(n_local):
        out_ref[e] = out[e * capacity : (e + 1) * capacity]


def raw_kernel(rows_ref, down_ref, out_ref):
    out_ref[0] = jnp.dot(rows_ref[...], down_ref[...], preferred_element_type=F32).astype(BF)


def factors(g, u):
    sig = 1.0 / (1.0 + jnp.exp(-g))
    return u * sig * (1.0 + g * (1.0 - sig)), g * sig


def share_kernel(place_ref, parts_ref, gate_ref, up_ref, raw_ref, delta_ref):
    quarter = raw_ref.shape[1]
    raw = parts_ref[0].astype(F32)
    for i in range(1, parts_ref.shape[0]):
        raw = raw + parts_ref[i].astype(F32)
    raw_ref[...] = raw.astype(BF)
    here = pl.ds(pl.multiple_of(place_ref[1] * quarter, quarter), quarter)
    for_gate, for_up = factors(gate_ref[:, here].astype(F32), up_ref[:, here].astype(F32))
    gate_delta = (raw * for_gate).astype(BF)
    up_delta = (raw * for_up).astype(BF)
    delta_ref[:, :quarter] = gate_delta
    delta_ref[:, quarter:] = up_delta


def grads_kernel(own, place_ref, delta_ref, *refs):
    out_ref = refs[-1]
    n_z, n_y = out_ref.shape[:2]

    def block(x):
        res = lax.dot_general(
            x, delta_ref[...], (((0,), (0,)), ((), ())), preferred_element_type=F32
        )
        for i in range(n_y * n_z):
            piece = res[i * own : (i + 1) * own]
            tall = jnp.concatenate(
                [piece[:, c * 128 : (c + 1) * 128] for c in range(piece.shape[1] // 128)], axis=0
            )
            out_ref[i % n_z, i // n_z, 0] = tall.astype(BF)

    if len(refs) == 4:
        block(jnp.concatenate([refs[0][...], refs[1][...]], axis=0))
        return
    step = pl.program_id(0)

    @pl.when(step == 0)
    def _():
        block(refs[0][...])

    for k in (1, 2):

        @pl.when(step == k)
        def _(k=k):
            block(jnp.concatenate([refs[2 * k - 1][...], refs[2 * k][...]], axis=0))


def input_kernel(capacity, place_ref, raw_ref, gate_ref, up_ref, wg_ref, wu_ref, out_ref, total, side):
    step = pl.program_id(0)
    raw = raw_ref[0].astype(F32)
    u = up_ref[...].astype(F32)
    for_gate, for_up = factors(gate_ref[...].astype(F32), u)
    up_delta = raw * for_up
    dims = (((1,), (1,)), ((), ()))
    term = lax.dot_general(
        (raw * for_gate).astype(BF), wg_ref[...], dims, preferred_element_type=F32
    ) + lax.dot_general(up_delta.astype(BF), wu_ref[...], dims, preferred_element_type=F32)
    dgate = jnp.broadcast_to(jnp.sum(up_delta * u, axis=1, keepdims=True), side.shape)

    @pl.when(step == 0)
    def _():
        total[...] = term
        side[...] = dgate

    @pl.when(step > 0)
    def _():
        total[...] += term
        side[...] += dgate

    @pl.when(step == pl.num_programs(0) - 1)
    def _():
        feat = total.shape[1]
        rest = out_ref.shape[2] - feat
        for k in range(out_ref.shape[0]):
            to = jnp.bitwise_xor(place_ref[2], k)
            rows = pl.ds(pl.multiple_of(to * capacity, 8), capacity)
            out_ref[k, :, :feat] = total[rows, :].astype(BF)
            out_ref[k, :, feat:] = side[rows, :rest].astype(BF)


def combine_kernel(n_local, capacity, place_ref, routes_ref, gates_ref, *rest):
    back_refs, (rows_ref, grads_ref) = rest[:-2], rest[-2:]
    masks = [
        jnp.where(m, 1.0, 0.0).astype(BF)
        for m in picks_of(routes_ref[...].T, n_local, capacity, place_ref[2])
    ]
    feat = rows_ref.shape[0]
    back = jnp.concatenate([r[...] for r in back_refs], axis=0)
    rows_ref[...] = lax.dot_general(
        back[:, :feat], sum(masks[1:], masks[0]), (((0,), (1,)), ((), ())), preferred_element_type=F32
    ).astype(BF)
    tail = back[:, back.shape[1] - 128 :]
    gates = gates_ref[...].astype(F32)
    for k, m in enumerate(masks):
        sums = lax.dot_general(
            tail, m, (((0,), (1,)), ((), ())), preferred_element_type=F32
        )[127:128]
        grads_ref[k : k + 1, :] = (sums / gates[k : k + 1, :]).astype(BF)


def final_kernel(n_copies, own, parts_ref, gate_ref, up_ref):
    copies, n_node = parts_ref.shape[0], parts_ref.shape[1]
    for x in range(n_node):
        total = parts_ref[0, x].astype(F32)
        for i in range(1, copies):
            total = total + parts_ref[i, x].astype(F32)
        total = total * (1.0 / n_copies)
        per = total.shape[0] // own // 2
        for c in range(2 * per):
            out = gate_ref if c < per else up_ref
            out[:, x * per + c % per, :] = total[c * own : (c + 1) * own]


def params(mib=32, **more):
    return pltpu.CompilerParams(vmem_limit_bytes=mib * MIB, **more)


def ring(x, axis, step):
    n = lax.axis_size(axis)
    return lax.ppermute(x, axis, [(i, (i + step) % n) for i in range(n)])


SMEM = pl.BlockSpec(memory_space=pltpu.SMEM)
VMEM = pl.BlockSpec(memory_space=pltpu.VMEM)


def local(token_grads, routes, gates, expert_inputs, gate_pre, up_pre, w_gate, w_up, w_down):
    tokens, top = routes.shape
    n_local = lax.axis_size("local")
    n_node = lax.axis_size("node")
    n_z, n_y = lax.axis_size("z"), lax.axis_size("y")
    n_copies = n_y * n_z
    capacity = expert_inputs.shape[3]
    feat = token_grads.shape[1]
    hidden = gate_pre.shape[4]
    quarter = hidden // n_node
    slots = n_local * capacity
    own = feat // n_copies
    wide = -(-(feat + 1) // 128) * 128
    place = jnp.stack([lax.axis_index(a) for a in ("z", "node", "local")]).astype(jnp.int32)
    gate_rows = gate_pre.reshape(slots, hidden)
    up_rows = up_pre.reshape(slots, hidden)
    x_rows = expert_inputs.reshape(slots, feat)

    outgoing = pl.pallas_call(
        functools.partial(dispatch_kernel, n_local, capacity),
        in_specs=[pl.BlockSpec(memory_space=pl.ANY)] * 3,
        scratch_shapes=[
            pltpu.VMEM((top, tokens), jnp.int32),
            pltpu.VMEM((top, tokens), BF),
            pltpu.VMEM((feat, tokens), BF),
            pltpu.SemaphoreType.DMA((3,)),
        ],
        out_shape=jax.ShapeDtypeStruct((n_local, capacity, feat), BF),
        compiler_params=params(56),
        name="dispatch",
    )(routes.T, gates.T, token_grads.T)
    arrived = lax.all_to_all(outgoing, "local", split_axis=0, concat_axis=0, tiled=True)

    half = slots // 2
    x_rows, _ = lax.optimization_barrier((x_rows, outgoing))
    x_halves = (x_rows[:half], x_rows[half:])
    x_prev = [ring(x, "node", 1) for x in x_halves]
    x_next = [ring(x, "node", -1) for x in x_halves]

    raw_parts = pl.pallas_call(
        raw_kernel,
        grid=(n_node,),
        in_specs=[
            pl.BlockSpec((slots, feat), lambda i: (0, 0)),
            pl.BlockSpec((feat, quarter), lambda i: (0, i)),
        ],
        out_specs=pl.BlockSpec((1, slots, quarter), lambda i: (i, 0, 0)),
        out_shape=jax.ShapeDtypeStruct((n_node, slots, quarter), BF),
        compiler_params=params(),
        name="raw",
    )(arrived.reshape(slots, feat), w_down[0].T)
    raw_shares = lax.all_to_all(raw_parts, "node", split_axis=0, concat_axis=0, tiled=True)

    x_prev[0], x_next[1], _ = lax.optimization_barrier((x_prev[0], x_next[1], raw_parts))
    x_across = (ring(x_prev[0], "node", 1), ring(x_next[1], "node", -1))

    raw_share, deltas = pl.pallas_call(
        share_kernel,
        in_specs=[SMEM, VMEM, VMEM, VMEM],
        out_shape=[
            jax.ShapeDtypeStruct((slots, quarter), BF),
            jax.ShapeDtypeStruct((slots, 2 * quarter), BF),
        ],
        compiler_params=params(),
        name="share",
    )(place, raw_shares, gate_rows, up_rows)

    tall = own * 2 * quarter // 128
    def products(count, pieces, turn, before):
        return pl.pallas_call(
            functools.partial(grads_kernel, own),
            grid_spec=pltpu.PrefetchScalarGridSpec(
                num_scalar_prefetch=1,
                grid=(count,),
                in_specs=[pl.BlockSpec((slots, 2 * quarter), lambda i, p: (0, 0))]
                + [pl.BlockSpec(x.shape, lambda i, p: (0, 0)) for x in pieces]
                + [pl.BlockSpec(memory_space=pl.ANY)] * len(before),
                out_specs=pl.BlockSpec(
                    (n_z, n_y, 1, tall, 128),
                    lambda i, p: (0, 0, (p[1] + turn(i)) % n_node, 0, 0),
                ),
            ),
            out_shape=jax.ShapeDtypeStruct((n_z, n_y, n_node, tall, 128), BF),
            input_output_aliases={2 + len(pieces): 0} if before else {},
            compiler_params=params(56),
            name="grads",
        )(place, deltas, *pieces, *before)

    grads = products(3, (x_rows, *x_prev, *x_next), lambda i: jnp.where(i < 2, 3 * i, 1), ())
    grads = products(1, x_across, lambda i: 2 + i, (grads,))
    z_sum = lax.psum_scatter(
        grads.reshape(n_z * n_y * n_node * tall, 128), "z", scatter_dimension=0, tiled=True
    )

    raw_share, _ = lax.optimization_barrier((raw_share, grads))
    raw = lax.all_gather(raw_share, "node", axis=0, tiled=False)
    slot_input = pl.pallas_call(
        functools.partial(input_kernel, capacity),
        grid=(n_node,),
        in_specs=[
            SMEM,
            pl.BlockSpec((1, slots, quarter), lambda i: (i, 0, 0)),
            pl.BlockSpec((slots, quarter), lambda i: (0, i)),
            pl.BlockSpec((slots, quarter), lambda i: (0, i)),
            pl.BlockSpec((feat, quarter), lambda i: (0, i)),
            pl.BlockSpec((feat, quarter), lambda i: (0, i)),
        ],
        out_specs=pl.BlockSpec((n_local, capacity, wide), lambda i: (0, 0, 0)),
        out_shape=jax.ShapeDtypeStruct((n_local, capacity, wide), BF),
        scratch_shapes=[pltpu.VMEM((slots, feat), F32), pltpu.VMEM((slots, 128), F32)],
        compiler_params=params(),
        name="slot_input",
    )(place, raw, gate_rows, up_rows, w_gate[0], w_up[0])
    back = [slot_input[0]] + [
        lax.ppermute(slot_input[k], "local", [(i, i ^ k) for i in range(n_local)])
        for k in range(1, n_local)
    ]
    input_grads, gate_grads = pl.pallas_call(
        functools.partial(combine_kernel, n_local, capacity),
        in_specs=[SMEM] + [VMEM] * (2 + n_local),
        out_shape=[
            jax.ShapeDtypeStruct((feat, tokens), BF),
            jax.ShapeDtypeStruct((top, tokens), BF),
        ],
        compiler_params=params(),
        name="combine",
    )(place, routes.T, gates.T, *back)

    z_sum, input_grads, gate_grads = lax.optimization_barrier((z_sum, input_grads, gate_grads))
    parts = lax.all_to_all(
        z_sum.reshape(n_y * n_node, tall, 128),
        ("y", "node"),
        split_axis=0,
        concat_axis=0,
        tiled=True,
    )
    gate_sum, up_sum = pl.pallas_call(
        functools.partial(final_kernel, n_copies, own),
        out_shape=[jax.ShapeDtypeStruct((own, hidden // 128, 128), F32)] * 2,
        compiler_params=params(),
        name="final",
    )(parts.reshape(n_y, n_node, tall, 128))
    rows = own * hidden // 128
    return (
        input_grads.T,
        gate_grads.T,
        gate_sum.reshape(1, 1, rows, 128),
        up_sum.reshape(1, 1, rows, 128),
    )


def solution(mesh):
    shape = mesh.devices.shape
    cut = Mesh(mesh.devices.reshape(*CUT, shape[1], shape[2]), ("y", "z", "node", "local"))
    replica = ("y", "z")
    placed = (
        P((*replica, "local"), "node"),
        P((*replica, "local"), None),
        P((*replica, "local"), None),
        P(replica, "local", None, None, "node"),
        P(replica, "local", None, None, None),
        P(replica, "local", None, None, None),
        P("local", "node", None),
        P("local", "node", None),
        P("local", None, "node"),
    )
    return jax.shard_map(
        local,
        mesh=cut,
        in_specs=placed,
        out_specs=(
            P((*replica, "local"), "node"),
            P((*replica, "local"), None),
            P("local", "node", replica, None),
            P("local", "node", replica, None),
        ),
        check_vma=False,
    )
```

```python
import functools

import jax
import jax.numpy as jnp
from jax import lax
from jax.experimental import pallas as pl
from jax.experimental.pallas import tpu as pltpu
from jax.sharding import Mesh
from jax.sharding import PartitionSpec as P

BF = jnp.bfloat16
F32 = jnp.float32
MIB = 1 << 20


CUT = (4, 12)


def picks_of(routes, n_local, capacity, turn=None):
    tokens, top = routes.shape
    lanes = lax.broadcasted_iota(jnp.int32, (tokens, 128), 1)
    named = [(lanes == routes[:, k : k + 1]) for k in range(top)]
    total = sum(jnp.where(n, 1.0, 0.0) for n in named).astype(BF)
    rows = lax.broadcasted_iota(jnp.int32, (tokens, tokens), 0)
    cols = lax.broadcasted_iota(jnp.int32, (tokens, tokens), 1)
    earlier = jnp.where(cols < rows, 1.0, 0.0).astype(BF)
    before = jnp.dot(earlier, total, preferred_element_type=F32)
    slots = lax.broadcasted_iota(jnp.int32, (tokens, n_local * capacity), 1)
    block = routes if turn is None else jnp.bitwise_xor(routes, turn)
    masks = []
    for k in range(top):
        slot = jnp.sum(jnp.where(named[k], before, 0.0), axis=1, keepdims=True)
        masks.append(slots == block[:, k : k + 1] * capacity + slot.astype(jnp.int32))
    return masks


def dispatch_kernel(
    n_local, capacity, routes_in, gates_in, rows_in, out_ref, routes_ref, gates_ref, rows_ref, sems
):
    copies = [
        pltpu.make_async_copy(routes_in, routes_ref, sems.at[0]),
        pltpu.make_async_copy(gates_in, gates_ref, sems.at[1]),
        pltpu.make_async_copy(rows_in, rows_ref, sems.at[2]),
    ]
    for copy in copies:
        copy.start()
    copies[0].wait()
    masks = picks_of(routes_ref[...].T, n_local, capacity)
    copies[1].wait()
    gates = gates_ref[...].astype(F32).T
    scaled = sum(jnp.where(m, gates[:, k : k + 1], 0.0) for k, m in enumerate(masks)).astype(BF)
    copies[2].wait()
    out = lax.dot_general(
        scaled, rows_ref[...], (((0,), (1,)), ((), ())), preferred_element_type=F32
    ).astype(BF)
    for e in range(n_local):
        out_ref[e] = out[e * capacity : (e + 1) * capacity]


def raw_kernel(rows_ref, down_ref, out_ref):
    out_ref[0] = jnp.dot(rows_ref[...], down_ref[...], preferred_element_type=F32).astype(BF)


def factors(g, u):
    sig = 1.0 / (1.0 + jnp.exp(-g))
    return u * sig * (1.0 + g * (1.0 - sig)), g * sig


def share_kernel(place_ref, parts_ref, gate_ref, up_ref, raw_ref, delta_ref):
    quarter = raw_ref.shape[1]
    raw = parts_ref[0].astype(F32)
    for i in range(1, parts_ref.shape[0]):
        raw = raw + parts_ref[i].astype(F32)
    raw_ref[...] = raw.astype(BF)
    here = pl.ds(pl.multiple_of(place_ref[1] * quarter, quarter), quarter)
    for_gate, for_up = factors(gate_ref[:, here].astype(F32), up_ref[:, here].astype(F32))
    gate_delta = (raw * for_gate).astype(BF)
    up_delta = (raw * for_up).astype(BF)
    delta_ref[:, :quarter] = gate_delta
    delta_ref[:, quarter:] = up_delta


def grads_kernel(own, groups, turns, place_ref, delta_ref, *refs):
    out_ref, held, sems = refs[-3:]
    n_z, n_y, n_node = out_ref.shape[:3]
    copies = []
    for k, (group, turn) in enumerate(zip(groups, turns)):
        slot = k % held.shape[0]
        if k >= held.shape[0]:
            copies[k - held.shape[0]].wait()
        x = jnp.concatenate([refs[i][...] for i in group], axis=0)
        res = lax.dot_general(
            x, delta_ref[...], (((0,), (0,)), ((), ())), preferred_element_type=F32
        )
        for i in range(n_y * n_z):
            piece = res[i * own : (i + 1) * own]
            tall = jnp.concatenate(
                [piece[:, c * 128 : (c + 1) * 128] for c in range(piece.shape[1] // 128)], axis=0
            )
            held[slot, i % n_z, i // n_z] = tall.astype(BF)
        to = lax.rem(place_ref[1] + turn, n_node)
        copies.append(
            pltpu.make_async_copy(held.at[slot], out_ref.at[:, :, to], sems.at[slot])
        )
        copies[k].start()
    for copy in copies[-held.shape[0] :]:
        copy.wait()


def input_kernel(capacity, place_ref, raw_ref, gate_ref, up_ref, wg_ref, wu_ref, out_ref, total, side):
    step = pl.program_id(0)
    raw = raw_ref[0].astype(F32)
    u = up_ref[...].astype(F32)
    for_gate, for_up = factors(gate_ref[...].astype(F32), u)
    up_delta = raw * for_up
    dims = (((1,), (1,)), ((), ()))
    term = lax.dot_general(
        (raw * for_gate).astype(BF), wg_ref[...], dims, preferred_element_type=F32
    ) + lax.dot_general(up_delta.astype(BF), wu_ref[...], dims, preferred_element_type=F32)
    dgate = jnp.broadcast_to(jnp.sum(up_delta * u, axis=1, keepdims=True), side.shape)

    @pl.when(step == 0)
    def _():
        total[...] = term
        side[...] = dgate

    @pl.when(step > 0)
    def _():
        total[...] += term
        side[...] += dgate

    @pl.when(step == pl.num_programs(0) - 1)
    def _():
        feat = total.shape[1]
        rest = out_ref.shape[2] - feat
        for k in range(out_ref.shape[0]):
            to = jnp.bitwise_xor(place_ref[2], k)
            rows = pl.ds(pl.multiple_of(to * capacity, 8), capacity)
            out_ref[k, :, :feat] = total[rows, :].astype(BF)
            out_ref[k, :, feat:] = side[rows, :rest].astype(BF)


def combine_kernel(n_local, capacity, place_ref, routes_ref, gates_ref, *rest):
    back_refs, (rows_ref, grads_ref) = rest[:-2], rest[-2:]
    masks = [
        jnp.where(m, 1.0, 0.0).astype(BF)
        for m in picks_of(routes_ref[...].T, n_local, capacity, place_ref[2])
    ]
    feat = rows_ref.shape[0]
    back = jnp.concatenate([r[...] for r in back_refs], axis=0)
    rows_ref[...] = lax.dot_general(
        back[:, :feat], sum(masks[1:], masks[0]), (((0,), (1,)), ((), ())), preferred_element_type=F32
    ).astype(BF)
    tail = back[:, back.shape[1] - 128 :]
    gates = gates_ref[...].astype(F32)
    for k, m in enumerate(masks):
        sums = lax.dot_general(
            tail, m, (((0,), (1,)), ((), ())), preferred_element_type=F32
        )[127:128]
        grads_ref[k : k + 1, :] = (sums / gates[k : k + 1, :]).astype(BF)


def final_kernel(n_copies, own, parts_ref, gate_ref, up_ref):
    copies, n_node = parts_ref.shape[0], parts_ref.shape[1]
    for x in range(n_node):
        total = parts_ref[0, x].astype(F32)
        for i in range(1, copies):
            total = total + parts_ref[i, x].astype(F32)
        total = total * (1.0 / n_copies)
        per = total.shape[0] // own // 2
        for c in range(2 * per):
            out = gate_ref if c < per else up_ref
            out[:, x * per + c % per, :] = total[c * own : (c + 1) * own]


def params(mib=32, **more):
    return pltpu.CompilerParams(vmem_limit_bytes=mib * MIB, **more)


def in_hbm(x):
    return pltpu.with_memory_space_constraint(x, pltpu.HBM)


def ring(x, axis, step):
    n = lax.axis_size(axis)
    return lax.ppermute(x, axis, [(i, (i + step) % n) for i in range(n)])


SMEM = pl.BlockSpec(memory_space=pltpu.SMEM)
VMEM = pl.BlockSpec(memory_space=pltpu.VMEM)
HBM = pl.BlockSpec(memory_space=pltpu.HBM)


def local(token_grads, routes, gates, expert_inputs, gate_pre, up_pre, w_gate, w_up, w_down):
    tokens, top = routes.shape
    n_local = lax.axis_size("local")
    n_node = lax.axis_size("node")
    n_z, n_y = lax.axis_size("z"), lax.axis_size("y")
    n_copies = n_y * n_z
    capacity = expert_inputs.shape[3]
    feat = token_grads.shape[1]
    hidden = gate_pre.shape[4]
    quarter = hidden // n_node
    slots = n_local * capacity
    own = feat // n_copies
    wide = -(-(feat + 1) // 128) * 128
    place = jnp.stack([lax.axis_index(a) for a in ("z", "node", "local")]).astype(jnp.int32)
    gate_rows = gate_pre.reshape(slots, hidden)
    up_rows = up_pre.reshape(slots, hidden)
    x_rows = expert_inputs.reshape(slots, feat)

    outgoing = pl.pallas_call(
        functools.partial(dispatch_kernel, n_local, capacity),
        in_specs=[HBM] * 3,
        scratch_shapes=[
            pltpu.VMEM((top, tokens), jnp.int32),
            pltpu.VMEM((top, tokens), BF),
            pltpu.VMEM((feat, tokens), BF),
            pltpu.SemaphoreType.DMA((3,)),
        ],
        out_shape=jax.ShapeDtypeStruct((n_local, capacity, feat), BF),
        compiler_params=params(),
        name="dispatch",
    )(*(in_hbm(a.T) for a in (routes, gates, token_grads)))
    arrived = lax.all_to_all(outgoing, "local", split_axis=0, concat_axis=0, tiled=True)

    half = slots // 2
    x_rows, _ = lax.optimization_barrier((x_rows, outgoing))
    x_halves = (x_rows[:half], x_rows[half:])
    x_prev = [ring(x, "node", 1) for x in x_halves]
    x_next = [ring(x, "node", -1) for x in x_halves]

    raw_parts = pl.pallas_call(
        raw_kernel,
        grid=(n_node,),
        in_specs=[
            pl.BlockSpec((slots, feat), lambda i: (0, 0)),
            pl.BlockSpec((feat, quarter), lambda i: (0, i)),
        ],
        out_specs=pl.BlockSpec((1, slots, quarter), lambda i: (i, 0, 0)),
        out_shape=jax.ShapeDtypeStruct((n_node, slots, quarter), BF),
        compiler_params=params(),
        name="raw",
    )(arrived.reshape(slots, feat), in_hbm(w_down[0].T))
    raw_shares = lax.all_to_all(raw_parts, "node", split_axis=0, concat_axis=0, tiled=True)

    x_prev[0], x_next[1], _ = lax.optimization_barrier((x_prev[0], x_next[1], raw_parts))
    x_across = (ring(x_prev[0], "node", 1), ring(x_next[1], "node", -1))

    raw_share, deltas = pl.pallas_call(
        share_kernel,
        in_specs=[SMEM, VMEM, VMEM, VMEM],
        out_shape=[
            jax.ShapeDtypeStruct((slots, quarter), BF),
            jax.ShapeDtypeStruct((slots, 2 * quarter), BF),
        ],
        compiler_params=params(),
        name="share",
    )(place, raw_shares, gate_rows, up_rows)

    tall = own * 2 * quarter // 128
    def products(groups, turns, before):
        pieces = [x for group in groups for x in group]
        at = iter(range(len(pieces)))
        count = min(2, len(groups))
        return pl.pallas_call(
            functools.partial(grads_kernel, own, [[next(at) for _ in g] for g in groups], turns),
            in_specs=[SMEM] + [VMEM] * (1 + len(pieces)) + [HBM] * len(before),
            out_specs=HBM,
            out_shape=pltpu.HBM((n_z, n_y, n_node, tall, 128), BF),
            scratch_shapes=[
                pltpu.VMEM((count, n_z, n_y, tall, 128), BF),
                pltpu.SemaphoreType.DMA((count,)),
            ],
            input_output_aliases={2 + len(pieces): 0} if before else {},
            compiler_params=params(24),
            name="grads",
        )(place, deltas, *pieces, *before)

    grads = products(((x_rows,), x_prev, x_next), (0, n_node - 1, 1), ())
    grads = products((x_across,), (2,), (grads,))
    z_sum = lax.psum_scatter(
        grads.reshape(n_z * n_y * n_node * tall, 128), "z", scatter_dimension=0, tiled=True
    )

    raw_share, _ = lax.optimization_barrier((raw_share, grads))
    raw = lax.all_gather(raw_share, "node", axis=0, tiled=False)
    slot_input = pl.pallas_call(
        functools.partial(input_kernel, capacity),
        grid=(n_node,),
        in_specs=[
            SMEM,
            pl.BlockSpec((1, slots, quarter), lambda i: (i, 0, 0)),
            pl.BlockSpec((slots, quarter), lambda i: (0, i)),
            pl.BlockSpec((slots, quarter), lambda i: (0, i)),
            pl.BlockSpec((feat, quarter), lambda i: (0, i)),
            pl.BlockSpec((feat, quarter), lambda i: (0, i)),
        ],
        out_specs=pl.BlockSpec((n_local, capacity, wide), lambda i: (0, 0, 0)),
        out_shape=jax.ShapeDtypeStruct((n_local, capacity, wide), BF),
        scratch_shapes=[pltpu.VMEM((slots, feat), F32), pltpu.VMEM((slots, 128), F32)],
        compiler_params=params(),
        name="slot_input",
    )(place, raw, gate_rows, up_rows, w_gate[0], w_up[0])
    back = [slot_input[0]] + [
        lax.ppermute(slot_input[k], "local", [(i, i ^ k) for i in range(n_local)])
        for k in range(1, n_local)
    ]
    input_grads, gate_grads = pl.pallas_call(
        functools.partial(combine_kernel, n_local, capacity),
        in_specs=[SMEM] + [VMEM] * (2 + n_local),
        out_shape=[
            jax.ShapeDtypeStruct((feat, tokens), BF),
            jax.ShapeDtypeStruct((top, tokens), BF),
        ],
        compiler_params=params(),
        name="combine",
    )(place, routes.T, gates.T, *back)

    z_sum, input_grads, gate_grads = lax.optimization_barrier((z_sum, input_grads, gate_grads))
    parts = lax.all_to_all(
        z_sum.reshape(n_y * n_node, tall, 128),
        ("y", "node"),
        split_axis=0,
        concat_axis=0,
        tiled=True,
    )
    gate_sum, up_sum = pl.pallas_call(
        functools.partial(final_kernel, n_copies, own),
        out_shape=[jax.ShapeDtypeStruct((own, hidden // 128, 128), F32)] * 2,
        compiler_params=params(),
        name="final",
    )(parts.reshape(n_y, n_node, tall, 128))
    rows = own * hidden // 128
    return (
        input_grads.T,
        gate_grads.T,
        gate_sum.reshape(1, 1, rows, 128),
        up_sum.reshape(1, 1, rows, 128),
    )


def solution(mesh):
    shape = mesh.devices.shape
    cut = Mesh(mesh.devices.reshape(*CUT, shape[1], shape[2]), ("y", "z", "node", "local"))
    replica = ("y", "z")
    placed = (
        P((*replica, "local"), "node"),
        P((*replica, "local"), None),
        P((*replica, "local"), None),
        P(replica, "local", None, None, "node"),
        P(replica, "local", None, None, None),
        P(replica, "local", None, None, None),
        P("local", "node", None),
        P("local", "node", None),
        P("local", None, "node"),
    )
    return jax.shard_map(
        local,
        mesh=cut,
        in_specs=placed,
        out_specs=(
            P((*replica, "local"), "node"),
            P((*replica, "local"), None),
            P("local", "node", replica, None),
            P("local", "node", replica, None),
        ),
        check_vma=False,
    )
```

```python
import functools

import jax
import jax.numpy as jnp
from jax import lax
from jax.experimental import pallas as pl
from jax.experimental.pallas import tpu as pltpu
from jax.sharding import Mesh
from jax.sharding import PartitionSpec as P

BF = jnp.bfloat16
F32 = jnp.float32
MIB = 1 << 20


CUT = (4, 12)


def picks_of(routes, n_local, capacity, turn=None):
    tokens, top = routes.shape
    lanes = lax.broadcasted_iota(jnp.int32, (tokens, 128), 1)
    named = [(lanes == routes[:, k : k + 1]) for k in range(top)]
    total = sum(jnp.where(n, 1.0, 0.0) for n in named).astype(BF)
    rows = lax.broadcasted_iota(jnp.int32, (tokens, tokens), 0)
    cols = lax.broadcasted_iota(jnp.int32, (tokens, tokens), 1)
    earlier = jnp.where(cols < rows, 1.0, 0.0).astype(BF)
    before = jnp.dot(earlier, total, preferred_element_type=F32)
    slots = lax.broadcasted_iota(jnp.int32, (tokens, n_local * capacity), 1)
    block = routes if turn is None else jnp.bitwise_xor(routes, turn)
    masks = []
    for k in range(top):
        slot = jnp.sum(jnp.where(named[k], before, 0.0), axis=1, keepdims=True)
        masks.append(slots == block[:, k : k + 1] * capacity + slot.astype(jnp.int32))
    return masks


def dispatch_kernel(
    n_local, capacity, routes_in, gates_in, rows_in, out_ref, routes_ref, gates_ref, rows_ref, sems
):
    copies = [
        pltpu.make_async_copy(routes_in, routes_ref, sems.at[0]),
        pltpu.make_async_copy(gates_in, gates_ref, sems.at[1]),
        pltpu.make_async_copy(rows_in, rows_ref, sems.at[2]),
    ]
    for copy in copies:
        copy.start()
    copies[0].wait()
    masks = picks_of(routes_ref[...].T, n_local, capacity)
    copies[1].wait()
    gates = gates_ref[...].astype(F32).T
    scaled = sum(jnp.where(m, gates[:, k : k + 1], 0.0) for k, m in enumerate(masks)).astype(BF)
    copies[2].wait()
    out = lax.dot_general(
        scaled, rows_ref[...], (((0,), (1,)), ((), ())), preferred_element_type=F32
    ).astype(BF)
    for e in range(n_local):
        out_ref[e] = out[e * capacity : (e + 1) * capacity]


def raw_kernel(rows_ref, down_in, out_ref, down_ref, sems):
    count, _, quarter = down_ref.shape
    copies = [
        pltpu.make_async_copy(
            down_in.at[:, i * quarter : (i + 1) * quarter], down_ref.at[i], sems.at[i]
        )
        for i in range(count)
    ]
    for copy in copies:
        copy.start()
    rows = rows_ref[...]
    for i, copy in enumerate(copies):
        copy.wait()
        out_ref[i] = jnp.dot(rows, down_ref[i], preferred_element_type=F32).astype(BF)


def factors(g, u):
    sig = 1.0 / (1.0 + jnp.exp(-g))
    return u * sig * (1.0 + g * (1.0 - sig)), g * sig


def share_kernel(place_ref, parts_ref, gate_ref, up_ref, raw_ref, delta_ref):
    quarter = raw_ref.shape[1]
    raw = parts_ref[0].astype(F32)
    for i in range(1, parts_ref.shape[0]):
        raw = raw + parts_ref[i].astype(F32)
    raw_ref[...] = raw.astype(BF)
    here = pl.ds(pl.multiple_of(place_ref[1] * quarter, quarter), quarter)
    for_gate, for_up = factors(gate_ref[:, here].astype(F32), up_ref[:, here].astype(F32))
    gate_delta = (raw * for_gate).astype(BF)
    up_delta = (raw * for_up).astype(BF)
    delta_ref[:, :quarter] = gate_delta
    delta_ref[:, quarter:] = up_delta


def grads_kernel(own, groups, turns, place_ref, delta_ref, *refs):
    out_ref, held, sems = refs[-3:]
    n_z, n_y, n_node = out_ref.shape[:3]
    copies = []
    for k, (group, turn) in enumerate(zip(groups, turns)):
        slot = k % held.shape[0]
        if k >= held.shape[0]:
            copies[k - held.shape[0]].wait()
        x = jnp.concatenate([refs[i][...] for i in group], axis=0)
        res = lax.dot_general(
            x, delta_ref[...], (((0,), (0,)), ((), ())), preferred_element_type=F32
        )
        for i in range(n_y * n_z):
            piece = res[i * own : (i + 1) * own]
            tall = jnp.concatenate(
                [piece[:, c * 128 : (c + 1) * 128] for c in range(piece.shape[1] // 128)], axis=0
            )
            held[slot, i % n_z, i // n_z] = tall.astype(BF)
        to = lax.rem(place_ref[1] + turn, n_node)
        copies.append(
            pltpu.make_async_copy(held.at[slot], out_ref.at[:, :, to], sems.at[slot])
        )
        copies[k].start()
    for copy in copies[-held.shape[0] :]:
        copy.wait()


def input_kernel(capacity, place_ref, raw_ref, gate_ref, up_ref, wg_ref, wu_ref, out_ref, total, side):
    step = pl.program_id(0)
    raw = raw_ref[0].astype(F32)
    u = up_ref[...].astype(F32)
    for_gate, for_up = factors(gate_ref[...].astype(F32), u)
    up_delta = raw * for_up
    dims = (((1,), (1,)), ((), ()))
    term = lax.dot_general(
        (raw * for_gate).astype(BF), wg_ref[...], dims, preferred_element_type=F32
    ) + lax.dot_general(up_delta.astype(BF), wu_ref[...], dims, preferred_element_type=F32)
    dgate = jnp.broadcast_to(jnp.sum(up_delta * u, axis=1, keepdims=True), side.shape)

    @pl.when(step == 0)
    def _():
        total[...] = term
        side[...] = dgate

    @pl.when(step > 0)
    def _():
        total[...] += term
        side[...] += dgate

    @pl.when(step == pl.num_programs(0) - 1)
    def _():
        feat = total.shape[1]
        rest = out_ref.shape[2] - feat
        for k in range(out_ref.shape[0]):
            to = jnp.bitwise_xor(place_ref[2], k)
            rows = pl.ds(pl.multiple_of(to * capacity, 8), capacity)
            out_ref[k, :, :feat] = total[rows, :].astype(BF)
            out_ref[k, :, feat:] = side[rows, :rest].astype(BF)


def combine_kernel(n_local, capacity, place_ref, routes_ref, gates_ref, *rest):
    back_refs, (rows_ref, grads_ref) = rest[:-2], rest[-2:]
    masks = [
        jnp.where(m, 1.0, 0.0).astype(BF)
        for m in picks_of(routes_ref[...].T, n_local, capacity, place_ref[2])
    ]
    feat = rows_ref.shape[0]
    back = jnp.concatenate([r[...] for r in back_refs], axis=0)
    rows_ref[...] = lax.dot_general(
        back[:, :feat], sum(masks[1:], masks[0]), (((0,), (1,)), ((), ())), preferred_element_type=F32
    ).astype(BF)
    tail = back[:, back.shape[1] - 128 :]
    gates = gates_ref[...].astype(F32)
    for k, m in enumerate(masks):
        sums = lax.dot_general(
            tail, m, (((0,), (1,)), ((), ())), preferred_element_type=F32
        )[127:128]
        grads_ref[k : k + 1, :] = (sums / gates[k : k + 1, :]).astype(BF)


def final_kernel(n_copies, own, parts_ref, gate_ref, up_ref):
    copies, n_node = parts_ref.shape[0], parts_ref.shape[1]
    for x in range(n_node):
        total = parts_ref[0, x].astype(F32)
        for i in range(1, copies):
            total = total + parts_ref[i, x].astype(F32)
        total = total * (1.0 / n_copies)
        per = total.shape[0] // own // 2
        for c in range(2 * per):
            out = gate_ref if c < per else up_ref
            out[:, x * per + c % per, :] = total[c * own : (c + 1) * own]


def params(mib=32, **more):
    return pltpu.CompilerParams(vmem_limit_bytes=mib * MIB, **more)


def in_hbm(x):
    return pltpu.with_memory_space_constraint(x, pltpu.HBM)


def ring(x, axis, step):
    n = lax.axis_size(axis)
    return lax.ppermute(x, axis, [(i, (i + step) % n) for i in range(n)])


SMEM = pl.BlockSpec(memory_space=pltpu.SMEM)
VMEM = pl.BlockSpec(memory_space=pltpu.VMEM)
HBM = pl.BlockSpec(memory_space=pltpu.HBM)


def local(token_grads, routes, gates, expert_inputs, gate_pre, up_pre, w_gate, w_up, w_down):
    tokens, top = routes.shape
    n_local = lax.axis_size("local")
    n_node = lax.axis_size("node")
    n_z, n_y = lax.axis_size("z"), lax.axis_size("y")
    n_copies = n_y * n_z
    capacity = expert_inputs.shape[3]
    feat = token_grads.shape[1]
    hidden = gate_pre.shape[4]
    quarter = hidden // n_node
    slots = n_local * capacity
    own = feat // n_copies
    wide = -(-(feat + 1) // 128) * 128
    place = jnp.stack([lax.axis_index(a) for a in ("z", "node", "local")]).astype(jnp.int32)
    gate_rows = gate_pre.reshape(slots, hidden)
    up_rows = up_pre.reshape(slots, hidden)
    x_rows = expert_inputs.reshape(slots, feat)

    outgoing = pl.pallas_call(
        functools.partial(dispatch_kernel, n_local, capacity),
        in_specs=[HBM] * 3,
        scratch_shapes=[
            pltpu.VMEM((top, tokens), jnp.int32),
            pltpu.VMEM((top, tokens), BF),
            pltpu.VMEM((feat, tokens), BF),
            pltpu.SemaphoreType.DMA((3,)),
        ],
        out_shape=jax.ShapeDtypeStruct((n_local, capacity, feat), BF),
        compiler_params=params(),
        name="dispatch",
    )(*(in_hbm(a.T) for a in (routes, gates, token_grads)))
    arrived = lax.all_to_all(outgoing, "local", split_axis=0, concat_axis=0, tiled=True)

    half = slots // 2
    x_rows, _ = lax.optimization_barrier((x_rows, outgoing))
    x_halves = (x_rows[:half], x_rows[half:])
    x_prev = [ring(x, "node", 1) for x in x_halves]
    x_next = [ring(x, "node", -1) for x in x_halves]

    raw_parts = pl.pallas_call(
        raw_kernel,
        in_specs=[VMEM, HBM],
        scratch_shapes=[
            pltpu.VMEM((n_node, feat, quarter), BF),
            pltpu.SemaphoreType.DMA((n_node,)),
        ],
        out_shape=jax.ShapeDtypeStruct((n_node, slots, quarter), BF),
        compiler_params=params(),
        name="raw",
    )(arrived.reshape(slots, feat), in_hbm(w_down[0].T))
    raw_shares = lax.all_to_all(raw_parts, "node", split_axis=0, concat_axis=0, tiled=True)

    x_prev[0], x_next[1], _ = lax.optimization_barrier((x_prev[0], x_next[1], raw_parts))
    x_across = (ring(x_prev[0], "node", 1), ring(x_next[1], "node", -1))

    raw_share, deltas = pl.pallas_call(
        share_kernel,
        in_specs=[SMEM, VMEM, VMEM, VMEM],
        out_shape=[
            jax.ShapeDtypeStruct((slots, quarter), BF),
            jax.ShapeDtypeStruct((slots, 2 * quarter), BF),
        ],
        compiler_params=params(),
        name="share",
    )(place, raw_shares, gate_rows, up_rows)

    tall = own * 2 * quarter // 128
    def products(groups, turns, before):
        pieces = [x for group in groups for x in group]
        at = iter(range(len(pieces)))
        count = min(2, len(groups))
        return pl.pallas_call(
            functools.partial(grads_kernel, own, [[next(at) for _ in g] for g in groups], turns),
            in_specs=[SMEM] + [VMEM] * (1 + len(pieces)) + [HBM] * len(before),
            out_specs=HBM,
            out_shape=pltpu.HBM((n_z, n_y, n_node, tall, 128), BF),
            scratch_shapes=[
                pltpu.VMEM((count, n_z, n_y, tall, 128), BF),
                pltpu.SemaphoreType.DMA((count,)),
            ],
            input_output_aliases={2 + len(pieces): 0} if before else {},
            compiler_params=params(24),
            name="grads",
        )(place, deltas, *pieces, *before)

    grads = products(((x_rows,),), (0,), ())
    grads = products((x_prev, x_next), (n_node - 1, 1), (grads,))
    grads = products((x_across,), (2,), (grads,))
    z_sum = lax.psum_scatter(
        grads.reshape(n_z * n_y * n_node * tall, 128), "z", scatter_dimension=0, tiled=True
    )

    raw_share, _ = lax.optimization_barrier((raw_share, grads))
    raw = lax.all_gather(raw_share, "node", axis=0, tiled=False)
    slot_input = pl.pallas_call(
        functools.partial(input_kernel, capacity),
        grid=(n_node,),
        in_specs=[
            SMEM,
            pl.BlockSpec((1, slots, quarter), lambda i: (i, 0, 0)),
            pl.BlockSpec((slots, quarter), lambda i: (0, i)),
            pl.BlockSpec((slots, quarter), lambda i: (0, i)),
            pl.BlockSpec((feat, quarter), lambda i: (0, i)),
            pl.BlockSpec((feat, quarter), lambda i: (0, i)),
        ],
        out_specs=pl.BlockSpec((n_local, capacity, wide), lambda i: (0, 0, 0)),
        out_shape=jax.ShapeDtypeStruct((n_local, capacity, wide), BF),
        scratch_shapes=[pltpu.VMEM((slots, feat), F32), pltpu.VMEM((slots, 128), F32)],
        compiler_params=params(),
        name="slot_input",
    )(place, raw, gate_rows, up_rows, w_gate[0], w_up[0])
    back = [slot_input[0]] + [
        lax.ppermute(slot_input[k], "local", [(i, i ^ k) for i in range(n_local)])
        for k in range(1, n_local)
    ]
    input_grads, gate_grads = pl.pallas_call(
        functools.partial(combine_kernel, n_local, capacity),
        in_specs=[SMEM] + [VMEM] * (2 + n_local),
        out_shape=[
            jax.ShapeDtypeStruct((feat, tokens), BF),
            jax.ShapeDtypeStruct((top, tokens), BF),
        ],
        compiler_params=params(),
        name="combine",
    )(place, routes.T, gates.T, *back)

    z_sum, input_grads, gate_grads = lax.optimization_barrier((z_sum, input_grads, gate_grads))
    parts = lax.all_to_all(
        z_sum.reshape(n_y * n_node, tall, 128),
        ("y", "node"),
        split_axis=0,
        concat_axis=0,
        tiled=True,
    )
    gate_sum, up_sum = pl.pallas_call(
        functools.partial(final_kernel, n_copies, own),
        out_shape=[jax.ShapeDtypeStruct((own, hidden // 128, 128), F32)] * 2,
        compiler_params=params(),
        name="final",
    )(parts.reshape(n_y, n_node, tall, 128))
    rows = own * hidden // 128
    return (
        input_grads.T,
        gate_grads.T,
        gate_sum.reshape(1, 1, rows, 128),
        up_sum.reshape(1, 1, rows, 128),
    )


def solution(mesh):
    shape = mesh.devices.shape
    cut = Mesh(mesh.devices.reshape(*CUT, shape[1], shape[2]), ("y", "z", "node", "local"))
    replica = ("y", "z")
    placed = (
        P((*replica, "local"), "node"),
        P((*replica, "local"), None),
        P((*replica, "local"), None),
        P(replica, "local", None, None, "node"),
        P(replica, "local", None, None, None),
        P(replica, "local", None, None, None),
        P("local", "node", None),
        P("local", "node", None),
        P("local", None, "node"),
    )
    return jax.shard_map(
        local,
        mesh=cut,
        in_specs=placed,
        out_specs=(
            P((*replica, "local"), "node"),
            P((*replica, "local"), None),
            P("local", "node", replica, None),
            P("local", "node", replica, None),
        ),
        check_vma=False,
    )
```

```python
import functools

import jax
import jax.numpy as jnp
from jax import lax
from jax.experimental import pallas as pl
from jax.experimental.pallas import tpu as pltpu
from jax.sharding import Mesh
from jax.sharding import PartitionSpec as P

BF = jnp.bfloat16
F32 = jnp.float32
MIB = 1 << 20


CUT = (4, 12)


def picks_of(routes, n_local, capacity, turn=None):
    tokens, top = routes.shape
    lanes = lax.broadcasted_iota(jnp.int32, (tokens, 128), 1)
    named = [(lanes == routes[:, k : k + 1]) for k in range(top)]
    total = sum(jnp.where(n, 1.0, 0.0) for n in named).astype(BF)
    rows = lax.broadcasted_iota(jnp.int32, (tokens, tokens), 0)
    cols = lax.broadcasted_iota(jnp.int32, (tokens, tokens), 1)
    earlier = jnp.where(cols < rows, 1.0, 0.0).astype(BF)
    before = jnp.dot(earlier, total, preferred_element_type=F32)
    slots = lax.broadcasted_iota(jnp.int32, (tokens, n_local * capacity), 1)
    block = routes if turn is None else jnp.bitwise_xor(routes, turn)
    masks = []
    for k in range(top):
        slot = jnp.sum(jnp.where(named[k], before, 0.0), axis=1, keepdims=True)
        masks.append(slots == block[:, k : k + 1] * capacity + slot.astype(jnp.int32))
    return masks


def dispatch_kernel(
    n_local, capacity, routes_in, gates_in, rows_in, out_ref, routes_ref, gates_ref, rows_ref, sems
):
    copies = [
        pltpu.make_async_copy(routes_in, routes_ref, sems.at[0]),
        pltpu.make_async_copy(gates_in, gates_ref, sems.at[1]),
        pltpu.make_async_copy(rows_in, rows_ref, sems.at[2]),
    ]
    for copy in copies:
        copy.start()
    copies[0].wait()
    masks = picks_of(routes_ref[...].T, n_local, capacity)
    copies[1].wait()
    gates = gates_ref[...].astype(F32).T
    scaled = sum(jnp.where(m, gates[:, k : k + 1], 0.0) for k, m in enumerate(masks)).astype(BF)
    copies[2].wait()
    out = lax.dot_general(
        scaled, rows_ref[...], (((0,), (1,)), ((), ())), preferred_element_type=F32
    ).astype(BF)
    for e in range(n_local):
        out_ref[e] = out[e * capacity : (e + 1) * capacity]


def raw_kernel(rows_ref, down_in, out_ref, down_ref, sems):
    count, _, quarter = down_ref.shape
    copies = [
        pltpu.make_async_copy(
            down_in.at[:, i * quarter : (i + 1) * quarter], down_ref.at[i], sems.at[i]
        )
        for i in range(count)
    ]
    for copy in copies:
        copy.start()
    rows = rows_ref[...]
    for i, copy in enumerate(copies):
        copy.wait()
        out_ref[i] = jnp.dot(rows, down_ref[i], preferred_element_type=F32).astype(BF)


def factors(g, u):
    sig = 1.0 / (1.0 + jnp.exp(-g))
    return u * sig * (1.0 + g * (1.0 - sig)), g * sig


def share_kernel(place_ref, parts_ref, gate_ref, up_ref, raw_ref, delta_ref):
    quarter = raw_ref.shape[1]
    raw = parts_ref[0].astype(F32)
    for i in range(1, parts_ref.shape[0]):
        raw = raw + parts_ref[i].astype(F32)
    raw_ref[...] = raw.astype(BF)
    here = pl.ds(pl.multiple_of(place_ref[1] * quarter, quarter), quarter)
    for_gate, for_up = factors(gate_ref[:, here].astype(F32), up_ref[:, here].astype(F32))
    gate_delta = (raw * for_gate).astype(BF)
    up_delta = (raw * for_up).astype(BF)
    delta_ref[:, :quarter] = gate_delta
    delta_ref[:, quarter:] = up_delta


def grads_kernel(own, groups, turns, place_ref, delta_ref, *refs):
    out_ref, held, sems = refs[-3:]
    n_z, n_node, n_y = out_ref.shape[:3]
    copies = []
    for k, (group, turn) in enumerate(zip(groups, turns)):
        slot = k % held.shape[0]
        if k >= held.shape[0]:
            copies[k - held.shape[0]].wait()
        x = jnp.concatenate([refs[i][...] for i in group], axis=0)
        res = lax.dot_general(
            x, delta_ref[...], (((0,), (0,)), ((), ())), preferred_element_type=F32
        )
        for i in range(n_y * n_z):
            piece = res[i * own : (i + 1) * own]
            tall = jnp.concatenate(
                [piece[:, c * 128 : (c + 1) * 128] for c in range(piece.shape[1] // 128)], axis=0
            )
            held[slot, i % n_z, i // n_z] = tall.astype(BF)
        to = lax.rem(place_ref[1] + turn, n_node)
        copies.append(
            pltpu.make_async_copy(held.at[slot], out_ref.at[:, to], sems.at[slot])
        )
        copies[k].start()
    for copy in copies[-held.shape[0] :]:
        copy.wait()


def input_kernel(capacity, place_ref, raw_ref, gate_ref, up_ref, wg_ref, wu_ref, out_ref, total, side):
    step = pl.program_id(0)
    raw = raw_ref[0].astype(F32)
    u = up_ref[...].astype(F32)
    for_gate, for_up = factors(gate_ref[...].astype(F32), u)
    up_delta = raw * for_up
    dims = (((1,), (1,)), ((), ()))
    term = lax.dot_general(
        (raw * for_gate).astype(BF), wg_ref[...], dims, preferred_element_type=F32
    ) + lax.dot_general(up_delta.astype(BF), wu_ref[...], dims, preferred_element_type=F32)
    dgate = jnp.broadcast_to(jnp.sum(up_delta * u, axis=1, keepdims=True), side.shape)

    @pl.when(step == 0)
    def _():
        total[...] = term
        side[...] = dgate

    @pl.when(step > 0)
    def _():
        total[...] += term
        side[...] += dgate

    @pl.when(step == pl.num_programs(0) - 1)
    def _():
        feat = total.shape[1]
        rest = out_ref.shape[2] - feat
        for k in range(out_ref.shape[0]):
            to = jnp.bitwise_xor(place_ref[2], k)
            rows = pl.ds(pl.multiple_of(to * capacity, 8), capacity)
            out_ref[k, :, :feat] = total[rows, :].astype(BF)
            out_ref[k, :, feat:] = side[rows, :rest].astype(BF)


def combine_kernel(n_local, capacity, place_ref, routes_ref, gates_ref, *rest):
    back_refs, (rows_ref, grads_ref) = rest[:-2], rest[-2:]
    masks = [
        jnp.where(m, 1.0, 0.0).astype(BF)
        for m in picks_of(routes_ref[...].T, n_local, capacity, place_ref[2])
    ]
    feat = rows_ref.shape[0]
    back = jnp.concatenate([r[...] for r in back_refs], axis=0)
    rows_ref[...] = lax.dot_general(
        back[:, :feat], sum(masks[1:], masks[0]), (((0,), (1,)), ((), ())), preferred_element_type=F32
    ).astype(BF)
    tail = back[:, back.shape[1] - 128 :]
    gates = gates_ref[...].astype(F32)
    for k, m in enumerate(masks):
        sums = lax.dot_general(
            tail, m, (((0,), (1,)), ((), ())), preferred_element_type=F32
        )[127:128]
        grads_ref[k : k + 1, :] = (sums / gates[k : k + 1, :]).astype(BF)


def final_kernel(n_copies, own, parts_ref, gate_ref, up_ref):
    n_node, copies = parts_ref.shape[0], parts_ref.shape[1]
    for x in range(n_node):
        total = parts_ref[x, 0].astype(F32)
        for i in range(1, copies):
            total = total + parts_ref[x, i].astype(F32)
        total = total * (1.0 / n_copies)
        per = total.shape[0] // own // 2
        for c in range(2 * per):
            out = gate_ref if c < per else up_ref
            out[:, x * per + c % per, :] = total[c * own : (c + 1) * own]


def params(mib=32, **more):
    return pltpu.CompilerParams(vmem_limit_bytes=mib * MIB, **more)


def in_hbm(x):
    return pltpu.with_memory_space_constraint(x, pltpu.HBM)


def ring(x, axis, step):
    n = lax.axis_size(axis)
    return lax.ppermute(x, axis, [(i, (i + step) % n) for i in range(n)])


SMEM = pl.BlockSpec(memory_space=pltpu.SMEM)
VMEM = pl.BlockSpec(memory_space=pltpu.VMEM)
HBM = pl.BlockSpec(memory_space=pltpu.HBM)


def local(token_grads, routes, gates, expert_inputs, gate_pre, up_pre, w_gate, w_up, w_down):
    tokens, top = routes.shape
    n_local = lax.axis_size("local")
    n_node = lax.axis_size("node")
    n_z, n_y = lax.axis_size("z"), lax.axis_size("y")
    n_copies = n_y * n_z
    capacity = expert_inputs.shape[3]
    feat = token_grads.shape[1]
    hidden = gate_pre.shape[4]
    quarter = hidden // n_node
    slots = n_local * capacity
    own = feat // n_copies
    wide = -(-(feat + 1) // 128) * 128
    place = jnp.stack([lax.axis_index(a) for a in ("z", "node", "local")]).astype(jnp.int32)
    gate_rows = gate_pre.reshape(slots, hidden)
    up_rows = up_pre.reshape(slots, hidden)
    x_rows = expert_inputs.reshape(slots, feat)

    outgoing = pl.pallas_call(
        functools.partial(dispatch_kernel, n_local, capacity),
        in_specs=[HBM] * 3,
        scratch_shapes=[
            pltpu.VMEM((top, tokens), jnp.int32),
            pltpu.VMEM((top, tokens), BF),
            pltpu.VMEM((feat, tokens), BF),
            pltpu.SemaphoreType.DMA((3,)),
        ],
        out_shape=jax.ShapeDtypeStruct((n_local, capacity, feat), BF),
        compiler_params=params(),
        name="dispatch",
    )(*(in_hbm(a.T) for a in (routes, gates, token_grads)))
    arrived = lax.all_to_all(outgoing, "local", split_axis=0, concat_axis=0, tiled=True)

    half = slots // 2
    x_rows, _ = lax.optimization_barrier((x_rows, outgoing))
    x_halves = (x_rows[:half], x_rows[half:])
    x_prev = [ring(x, "node", 1) for x in x_halves]
    x_next = [ring(x, "node", -1) for x in x_halves]

    raw_parts = pl.pallas_call(
        raw_kernel,
        in_specs=[VMEM, HBM],
        scratch_shapes=[
            pltpu.VMEM((n_node, feat, quarter), BF),
            pltpu.SemaphoreType.DMA((n_node,)),
        ],
        out_shape=jax.ShapeDtypeStruct((n_node, slots, quarter), BF),
        compiler_params=params(),
        name="raw",
    )(arrived.reshape(slots, feat), in_hbm(w_down[0].T))
    raw_shares = lax.all_to_all(raw_parts, "node", split_axis=0, concat_axis=0, tiled=True)

    x_prev[0], x_next[1], _ = lax.optimization_barrier((x_prev[0], x_next[1], raw_parts))
    x_across = (ring(x_prev[0], "node", 1), ring(x_next[1], "node", -1))

    raw_share, deltas = pl.pallas_call(
        share_kernel,
        in_specs=[SMEM, VMEM, VMEM, VMEM],
        out_shape=[
            jax.ShapeDtypeStruct((slots, quarter), BF),
            jax.ShapeDtypeStruct((slots, 2 * quarter), BF),
        ],
        compiler_params=params(),
        name="share",
    )(place, raw_shares, gate_rows, up_rows)

    tall = own * 2 * quarter // 128
    def products(groups, turns, before):
        pieces = [x for group in groups for x in group]
        at = iter(range(len(pieces)))
        count = min(2, len(groups))
        return pl.pallas_call(
            functools.partial(grads_kernel, own, [[next(at) for _ in g] for g in groups], turns),
            in_specs=[SMEM] + [VMEM] * (1 + len(pieces)) + [HBM] * len(before),
            out_specs=HBM,
            out_shape=pltpu.HBM((n_z, n_node, n_y, tall, 128), BF),
            scratch_shapes=[
                pltpu.VMEM((count, n_z, n_y, tall, 128), BF),
                pltpu.SemaphoreType.DMA((count,)),
            ],
            input_output_aliases={2 + len(pieces): 0} if before else {},
            compiler_params=params(24),
            name="grads",
        )(place, deltas, *pieces, *before)

    grads = products(((x_rows,),), (0,), ())
    grads = products((x_prev, x_next), (n_node - 1, 1), (grads,))
    grads = products((x_across,), (2,), (grads,))
    z_sum = lax.psum_scatter(
        grads.reshape(n_z * n_y * n_node * tall, 128), "z", scatter_dimension=0, tiled=True
    )

    raw_share, _ = lax.optimization_barrier((raw_share, grads))
    raw = lax.all_gather(raw_share, "node", axis=0, tiled=False)
    slot_input = pl.pallas_call(
        functools.partial(input_kernel, capacity),
        grid=(n_node,),
        in_specs=[
            SMEM,
            pl.BlockSpec((1, slots, quarter), lambda i: (i, 0, 0)),
            pl.BlockSpec((slots, quarter), lambda i: (0, i)),
            pl.BlockSpec((slots, quarter), lambda i: (0, i)),
            pl.BlockSpec((feat, quarter), lambda i: (0, i)),
            pl.BlockSpec((feat, quarter), lambda i: (0, i)),
        ],
        out_specs=pl.BlockSpec((n_local, capacity, wide), lambda i: (0, 0, 0)),
        out_shape=jax.ShapeDtypeStruct((n_local, capacity, wide), BF),
        scratch_shapes=[pltpu.VMEM((slots, feat), F32), pltpu.VMEM((slots, 128), F32)],
        compiler_params=params(),
        name="slot_input",
    )(place, raw, gate_rows, up_rows, w_gate[0], w_up[0])
    back = [slot_input[0]] + [
        lax.ppermute(slot_input[k], "local", [(i, i ^ k) for i in range(n_local)])
        for k in range(1, n_local)
    ]
    input_grads, gate_grads = pl.pallas_call(
        functools.partial(combine_kernel, n_local, capacity),
        in_specs=[SMEM] + [VMEM] * (2 + n_local),
        out_shape=[
            jax.ShapeDtypeStruct((feat, tokens), BF),
            jax.ShapeDtypeStruct((top, tokens), BF),
        ],
        compiler_params=params(),
        name="combine",
    )(place, routes.T, gates.T, *back)

    z_sum, input_grads, gate_grads = lax.optimization_barrier((z_sum, input_grads, gate_grads))
    parts = lax.all_to_all(
        z_sum.reshape(n_node * n_y, tall, 128),
        ("node", "y"),
        split_axis=0,
        concat_axis=0,
        tiled=True,
    )
    gate_sum, up_sum = pl.pallas_call(
        functools.partial(final_kernel, n_copies, own),
        out_shape=[jax.ShapeDtypeStruct((own, hidden // 128, 128), F32)] * 2,
        compiler_params=params(),
        name="final",
    )(parts.reshape(n_node, n_y, tall, 128))
    rows = own * hidden // 128
    return (
        input_grads.T,
        gate_grads.T,
        gate_sum.reshape(1, 1, rows, 128),
        up_sum.reshape(1, 1, rows, 128),
    )


def solution(mesh):
    shape = mesh.devices.shape
    cut = Mesh(mesh.devices.reshape(*CUT, shape[1], shape[2]), ("y", "z", "node", "local"))
    replica = ("y", "z")
    placed = (
        P((*replica, "local"), "node"),
        P((*replica, "local"), None),
        P((*replica, "local"), None),
        P(replica, "local", None, None, "node"),
        P(replica, "local", None, None, None),
        P(replica, "local", None, None, None),
        P("local", "node", None),
        P("local", "node", None),
        P("local", None, "node"),
    )
    return jax.shard_map(
        local,
        mesh=cut,
        in_specs=placed,
        out_specs=(
            P((*replica, "local"), "node"),
            P((*replica, "local"), None),
            P("local", "node", replica, None),
            P("local", "node", replica, None),
        ),
        check_vma=False,
    )
```
